256 devices in a mesh: space: 32 (over z, x), tm: 8 (over y, core).
Axes of the slice: x: 4, y: 4, z: 8, core: 2. Of those that a mesh axis runs over, the one named last changes fastest.
Arguments:
- snapshots: bfloat16 [512, 1048576], P('tm', 'space'), may hold values from -6 to 6
- pod_basis: bfloat16 [68, 1048576], P(None, 'space'), may hold values from -0.005859375 to 0.005859375
- penalty: float32 [2415], replicated, may hold values from 0.05 to 1
Outputs:
- normal: float32 [2416, 2415], P('tm')
- rhs: float32 [2416, 68], P('tm')
- reduced_state: float32 [8, 64, 68], P('tm', 'space')
- state_rates: float32 [8, 64, 68], P('tm', 'space')
The draws below stay inside these ranges and needn't reach their ends.
All inputs are finite; a program needn't handle non-finite values.
Results may differ from the reference program's by a relative error of at most 0.0003.
Values may be sent and summed in bfloat16 or wider, within the bound.
A program may use at most 128 MiB of HBM per device.

```python
import math
import jax
import jax.numpy as jnp
import numpy as np
from jax import lax

R = 68
F = 2415
FP = 2416
SNAP_TM = 64
NSNAP = 512
DOFS = 1048576
N_TM = 8


def shard_levels(own_key, extent, shards, least, top_value):
    gain = 1.0
    for axis_at, blocks in shards:
        draws = jax.random.uniform(jax.random.fold_in(jax.random.fold_in(own_key, 6), axis_at), (blocks,), jnp.float32, least / len(shards), top_value / len(shards))
        gain = gain * jnp.repeat(jnp.exp(draws), extent[axis_at] // blocks).reshape((-1,) + (1,) * (len(extent) - 1 - axis_at))
    return gain


def normal_values(key, dims, spread, limit, cuts=(), dtype=jnp.bfloat16):
    gain = shard_levels(key, dims, cuts, -0.22, 0.18) if cuts else 1.0
    result = jax.random.normal(key, dims, jnp.float32) * spread * gain
    return jnp.minimum(jnp.maximum(result, -limit), limit).astype(dtype)


def setup_inputs(seed: int = 0) -> dict:
    key_list = jax.random.split(jax.random.key(seed), 4)
    snapshots = normal_values(key_list[0], (NSNAP, DOFS), 1.0, 6.0, ((0, 8), (1, 32)))
    pod_basis = normal_values(key_list[1], (R, DOFS), DOFS ** -0.5, 0.005859375, ((1, 32),))
    penalty = jnp.clip(jnp.exp(jax.random.uniform(key_list[2], (F,), jnp.float32, math.log(0.05), math.log(1.0))), 0.05, 1.0)
    return dict(snapshots=snapshots, pod_basis=pod_basis, penalty=penalty)


def features(reduced):
    rows_count, mode_count = reduced.shape
    upper_rows, upper_cols = np.triu_indices(mode_count)
    flat_index = (upper_rows * mode_count + upper_cols).astype(np.int32)
    outer_prod = (reduced[:, :, None] * reduced[:, None, :]).reshape(rows_count, mode_count * mode_count)
    quadratic = jnp.take(outer_prod, flat_index, axis=1)
    constant = jnp.ones((rows_count, 1), jnp.float32)
    return jnp.concatenate([constant, reduced, quadratic], axis=1)


def reference(snapshots, pod_basis, penalty):
    reduced = jnp.dot(snapshots, pod_basis.T, preferred_element_type=jnp.float32)
    centred = (reduced[2:] - reduced[:-2]) * 0.5
    first_rate = reduced[1] - reduced[0]
    last_rate = reduced[-1] - reduced[-2]
    rates = jnp.concatenate([first_rate[None], centred, last_rate[None]], axis=0)
    feature_all = features(reduced)
    gram = jnp.dot(feature_all.T, feature_all, precision=lax.Precision.HIGHEST, preferred_element_type=jnp.float32)
    normal = gram / NSNAP + jnp.diag(penalty)
    rhs = jnp.dot(feature_all.T, rates, precision=lax.Precision.HIGHEST, preferred_element_type=jnp.float32) / NSNAP
    normal = jnp.pad(normal, ((0, FP - F), (0, 0)))
    rhs = jnp.pad(rhs, ((0, FP - F), (0, 0)))
    return normal, rhs, reduced.reshape(N_TM, SNAP_TM, R), rates.reshape(N_TM, SNAP_TM, R)
```

```python
import functools

import jax
import jax.numpy as jnp
from jax import lax
from jax.experimental import pallas as pl
from jax.experimental.pallas import tpu as pltpu
from jax.sharding import PartitionSpec as P

R = 68
HALF = R // 2
F = 1 + R + R * (R + 1) // 2
ROWS = 2560
RATE_ROW = 2432
NX, NZ, NT = 4, 8, 8
CHUNKS = 8
MESH = pl.DeviceIdType.MESH
CONTRACT_LANES = (((1,), (1,)), ((), ()))


def quadratic_rows():
    starts, at = [], 1 + R
    for i in range(R):
        starts.append(at)
        at += R - i
    return starts


def project_and_share(
    snap_hbm, pod_hbm, out_ref, snap, pod, xbuf, zbuf, tbuf, load_sem, send_sem, recv_sem
):
    space, tm = lax.axis_index("space"), lax.axis_index("tm")
    z, x = space // NX, lax.rem(space, NX)
    x_peers = [(z * NX + lax.rem(x + k, NX), tm) for k in range(1, NX)]
    z_peers = [(lax.rem(z + k, NZ) * NX + x, tm) for k in range(1, NZ)]
    t_peers = [(space, lax.rem(tm + k, NT)) for k in range(1, NT)]

    width = snap_hbm.shape[1] // CHUNKS

    def loads(i):
        cols = pl.ds(i * width, width)
        return (
            pltpu.make_async_copy(snap_hbm.at[:, cols], snap.at[:, cols], load_sem.at[0, i]),
            pltpu.make_async_copy(pod_hbm.at[:, cols], pod.at[:, cols], load_sem.at[1, i]),
        )

    for i in range(CHUNKS):
        for copy in loads(i):
            copy.start()

    barrier = pltpu.get_barrier_semaphore()
    peers = z_peers + t_peers + x_peers
    for peer in peers:
        pl.semaphore_signal(barrier, inc=1, device_id=peer, device_id_type=MESH)

    total = jnp.zeros((R, snap_hbm.shape[0]), jnp.float32)
    for i in range(CHUNKS):
        for copy in loads(i):
            copy.wait()
        cols = slice(i * width, (i + 1) * width)
        total = total + lax.dot_general(
            pod[:, cols], snap[:, cols], CONTRACT_LANES, preferred_element_type=jnp.float32
        )
    packed = jnp.concatenate([total[:HALF], total[HALF:]], axis=1)

    pl.semaphore_wait(barrier, len(peers))

    def exchange(phase, buf, rank, peers):
        count = len(peers)
        for peer in peers:
            pltpu.make_async_remote_copy(
                src_ref=buf.at[rank],
                dst_ref=buf.at[rank],
                send_sem=send_sem.at[phase],
                recv_sem=recv_sem.at[phase],
                device_id=peer,
                device_id_type=MESH,
            ).start()
        slots = buf.at[pl.ds(0, count)]
        pltpu.make_async_copy(slots, slots, recv_sem.at[phase]).wait()

    xbuf[x] = packed
    exchange(0, xbuf, x, x_peers)
    zbuf[z] = (xbuf[0] + xbuf[1]) + (xbuf[2] + xbuf[3])
    exchange(1, zbuf, z, z_peers)
    tbuf[tm] = ((zbuf[0] + zbuf[1]) + (zbuf[2] + zbuf[3])) + (
        (zbuf[4] + zbuf[5]) + (zbuf[6] + zbuf[7])
    )
    exchange(2, tbuf, tm, t_peers)

    half_lane = lax.broadcasted_iota(jnp.int32, (HALF, 128), 1) < 64
    for y in range(NT // 2):
        a, b = tbuf[2 * y], tbuf[2 * y + 1]
        out_ref[y, 0:HALF] = jnp.where(half_lane, a, pltpu.roll(b, 64, 1))
        out_ref[y, HALF:R] = jnp.where(half_lane, pltpu.roll(a, 64, 1), b)

    for phase, (buf, peers) in enumerate(((xbuf, x_peers), (zbuf, z_peers), (tbuf, t_peers))):
        slots = buf.at[pl.ds(0, len(peers))]
        pltpu.make_async_copy(slots, slots, send_sem.at[phase]).wait()


def normal_equations(
    modes_ref, pen_ref, normal_ref, rhs_ref, state_ref, rate_ref, modes, rates, feat, hi, lo, own, turned, obuf, rbuf, sem
):
    space, tm = lax.axis_index("space"), lax.axis_index("tm")
    rows = normal_ref.shape[0]
    groups = modes_ref.shape[0]
    snaps = groups * 128

    modes[:, :R] = modes_ref[...]
    modes[:, R:80] = jnp.zeros((groups, 80 - R, 128), jnp.float32)
    feat[:, 0:1] = jnp.ones((groups, 1, 128), jnp.float32)
    feat[:, 1 : 1 + R] = modes[:, :R]
    for i, at in enumerate(quadratic_rows()):
        count = -(-(R - i) // 8) * 8
        feat[:, at : at + count] = modes[:, i : i + count] * modes[:, i : i + 1]
    feat[:, F:RATE_ROW] = jnp.zeros((groups, RATE_ROW - F, 128), jnp.float32)

    whole = jnp.concatenate([modes[y, :72] for y in range(groups)], axis=1)
    col = lax.broadcasted_iota(jnp.int32, (72, snaps), 1)
    first, last = col == 0, col == snaps - 1
    after = jnp.where(last, whole, pltpu.roll(whole, snaps - 1, 1))
    before = jnp.where(first, whole, pltpu.roll(whole, 1, 1))
    rate = (after - before) * jnp.where(first | last, 1.0, 0.5)
    for y in range(groups):
        rates[y, 0:72] = rate[:, y * 128 : (y + 1) * 128]
        rates[y, 72:128] = jnp.zeros((56, 128), jnp.float32)
        feat[y, RATE_ROW:ROWS] = rates[y]

    first_row = tm * rows
    padded = own.shape[0] // 2
    for y in range(groups):
        lanes = slice(y * 128, (y + 1) * 128)
        value = feat[y, pl.ds(first_row, padded)]
        high = value.astype(jnp.bfloat16)
        own[0:padded, lanes] = high
        own[padded : 2 * padded, lanes] = (value - high.astype(jnp.float32)).astype(jnp.bfloat16)

        def split(r, carry, y=y, lanes=lanes):
            at = pl.ds(pl.multiple_of(r * 64, 64), 64)
            value = feat[y, at]
            high = value.astype(jnp.bfloat16)
            hi[at, lanes] = high
            lo[at, lanes] = (value - high.astype(jnp.float32)).astype(jnp.bfloat16)
            return carry

        lax.fori_loop(0, ROWS // 64, split, 0, unroll=4)

    at = lax.rem(tm, 2) * 64 + 2 * space
    turned[0] = jnp.concatenate([modes[tm // 2], jnp.zeros((48, 128), jnp.float32)], axis=0).T
    turned[1] = rates[tm // 2].T
    state_ref[0] = turned[0, pl.ds(at, 2)][:, :R]
    rate_ref[0] = turned[1, pl.ds(at, 2)][:, :R]

    row = lax.broadcasted_iota(jnp.int32, (rows, 256), 0) + first_row
    col = lax.broadcasted_iota(jnp.int32, (rows, 256), 1)
    copies = []
    tiles = ROWS // 256
    for n in range(tiles):
        cols = slice(n * 256, (n + 1) * 256)
        both = lax.dot_general(own[...], hi[cols], CONTRACT_LANES, preferred_element_type=jnp.float32)
        small = lax.dot_general(own[:padded], lo[cols], CONTRACT_LANES, preferred_element_type=jnp.float32)
        gram = ((both[:padded] + both[padded:] + small) * (1.0 / snaps))[:rows]
        if n < tiles - 1:
            penalty = pen_ref[0:1, cols]
        else:
            rbuf[...] = gram[:, 128:256].T[:R]
            gram, row, col = gram[:, :128], row[:, :128], col[:, :128]
            penalty = jnp.concatenate([pen_ref[0:1, n * 256 : F], jnp.zeros((1, RATE_ROW - F), jnp.float32)], axis=1)
        gram = gram + jnp.where(row == col + n * 256, penalty, 0.0)
        if n < tiles - 1:
            obuf[:, cols] = gram
        else:
            cols = slice(n * 256, F)
            obuf[:, cols] = gram[:, : F - n * 256]
        copies.append(pltpu.make_async_copy(obuf.at[:, cols], normal_ref.at[:, cols], sem.at[n]))
        copies[-1].start()
    copies.append(pltpu.make_async_copy(rbuf, rhs_ref, sem.at[tiles]))
    copies[-1].start()
    for copy in copies:
        copy.wait()


def shards(snapshots, pod_basis, penalty):
    group, dofs = snapshots.shape
    hbm = pl.BlockSpec(memory_space=pltpu.HBM)
    vmem = pl.BlockSpec(memory_space=pltpu.VMEM)
    modes = pl.pallas_call(
        project_and_share,
        out_shape=jax.ShapeDtypeStruct((NT // 2, R, 128), jnp.float32),
        in_specs=[hbm, hbm],
        out_specs=vmem,
        scratch_shapes=[
            pltpu.VMEM((group, dofs), jnp.bfloat16),
            pltpu.VMEM((R, dofs), jnp.bfloat16),
            pltpu.VMEM((NX, HALF, 128), jnp.float32),
            pltpu.VMEM((NZ, HALF, 128), jnp.float32),
            pltpu.VMEM((NT, HALF, 128), jnp.float32),
            pltpu.SemaphoreType.DMA((2, CHUNKS)),
            pltpu.SemaphoreType.DMA((3,)),
            pltpu.SemaphoreType.DMA((3,)),
        ],
        compiler_params=pltpu.CompilerParams(
            collective_id=0, has_side_effects=True, vmem_limit_bytes=56 << 20
        ),
        name="project_and_share",
    )(snapshots, pod_basis)
    own_rows = (F + 1) // NT
    padded = -(-own_rows // 16) * 16
    groups = NT // 2
    normal, rhs, state, rates = pl.pallas_call(
        normal_equations,
        out_shape=[
            jax.ShapeDtypeStruct((own_rows, F), jnp.float32),
            jax.ShapeDtypeStruct((R, own_rows), jnp.float32),
            jax.ShapeDtypeStruct((1, 2, R), jnp.float32),
            jax.ShapeDtypeStruct((1, 2, R), jnp.float32),
        ],
        in_specs=[vmem, vmem],
        out_specs=[hbm, hbm, vmem, vmem],
        scratch_shapes=[
            pltpu.VMEM((groups, 80, 128), jnp.float32),
            pltpu.VMEM((groups, 128, 128), jnp.float32),
            pltpu.VMEM((groups, ROWS, 128), jnp.float32),
            pltpu.VMEM((ROWS, groups * 128), jnp.bfloat16),
            pltpu.VMEM((ROWS, groups * 128), jnp.bfloat16),
            pltpu.VMEM((2 * padded, groups * 128), jnp.bfloat16),
            pltpu.VMEM((2, 128, 128), jnp.float32),
            pltpu.VMEM((own_rows, F), jnp.float32),
            pltpu.VMEM((R, own_rows), jnp.float32),
            pltpu.SemaphoreType.DMA((ROWS // 256 + 1,)),
        ],
        compiler_params=pltpu.CompilerParams(vmem_limit_bytes=32 << 20),
        name="normal_equations",
    )(modes, penalty[None, :])
    return normal, rhs.T, state, rates


def solution(mesh):
    return jax.shard_map(
        shards,
        mesh=mesh,
        in_specs=(P("tm", "space"), P(None, "space"), P()),
        out_specs=(P("tm", None), P("tm", None), P("tm", "space", None), P("tm", "space", None)),
        check_vma=False,
    )
```

```python
import functools

import jax
import jax.numpy as jnp
from jax import lax
from jax.experimental import pallas as pl
from jax.experimental.pallas import tpu as pltpu
from jax.sharding import PartitionSpec as P

R = 68
HALF = R // 2
F = 1 + R + R * (R + 1) // 2
ROWS = 2560
RATE_ROW = 2432
EARLY = 2304
OWN = (F + 1) // 8
PAD = -(-OWN // 16) * 16
GROUPS = 4
NX, NZ, NT = 4, 8, 8
CHUNKS = 8
MESH = pl.DeviceIdType.MESH
CONTRACT_LANES = (((1,), (1,)), ((), ()))


def quadratic_rows():
    starts, at = [], 1 + R
    for i in range(R):
        starts.append(at)
        at += R - i
    return starts


def split(value):
    high = value.astype(jnp.bfloat16)
    return high, (value - high.astype(jnp.float32)).astype(jnp.bfloat16)


def products(own, hi, lo):
    both = lax.dot_general(own, hi, CONTRACT_LANES, preferred_element_type=jnp.float32)
    small = lax.dot_general(own[:PAD], lo, CONTRACT_LANES, preferred_element_type=jnp.float32)
    return both[:PAD] + both[PAD:] + small


def project_and_share(
    snap_hbm, pod_hbm, part_ref, own_ref, hi_ref, lo_ref, mine_ref,
    snap, pod, xbuf, zbuf, tbuf, modes, feat, turned, load_sem, send_sem, recv_sem
):
    space, tm = lax.axis_index("space"), lax.axis_index("tm")
    z, x = space // NX, lax.rem(space, NX)
    y, core = tm // 2, lax.rem(tm, 2)
    x_peers = [(z * NX + lax.rem(x + k, NX), tm) for k in range(1, NX)]
    z_peers = [(lax.rem(z + k, NZ) * NX + x, tm) for k in range(1, NZ)]
    chips = [lax.rem(y + k, GROUPS) for k in range(GROUPS)]
    sibling = (space, 2 * y + (1 - core))
    t_peers = [sibling] + [(space, 2 * chips[k] + c) for k in range(1, GROUPS) for c in range(2)]

    width = snap_hbm.shape[1] // CHUNKS

    def loads(i):
        cols = pl.ds(i * width, width)
        return (
            pltpu.make_async_copy(snap_hbm.at[:, cols], snap.at[:, cols], load_sem.at[0, i]),
            pltpu.make_async_copy(pod_hbm.at[:, cols], pod.at[:, cols], load_sem.at[1, i]),
        )

    for i in range(CHUNKS):
        for copy in loads(i):
            copy.start()

    barrier = pltpu.get_barrier_semaphore()
    peers = z_peers + t_peers + x_peers
    for peer in peers:
        pl.semaphore_signal(barrier, inc=1, device_id=peer, device_id_type=MESH)

    feat[:, 0:1] = jnp.ones((GROUPS, 1, 128), jnp.float32)
    modes[:, R:80] = jnp.zeros((GROUPS, 80 - R, 128), jnp.float32)

    total = jnp.zeros((R, snap_hbm.shape[0]), jnp.float32)
    for i in range(CHUNKS):
        for copy in loads(i):
            copy.wait()
        cols = slice(i * width, (i + 1) * width)
        total = total + lax.dot_general(
            pod[:, cols], snap[:, cols], CONTRACT_LANES, preferred_element_type=jnp.float32
        )
    packed = jnp.concatenate([total[:HALF], total[HALF:]], axis=1)

    pl.semaphore_wait(barrier, len(peers))

    def send(buf, rank, peer, phase):
        pltpu.make_async_remote_copy(
            src_ref=buf.at[rank],
            dst_ref=buf.at[rank],
            send_sem=send_sem.at[min(phase, 2)],
            recv_sem=recv_sem.at[phase],
            device_id=peer,
            device_id_type=MESH,
        ).start()

    def arrived(buf, at, count, sem):
        slots = buf.at[pl.ds(at, count)]
        pltpu.make_async_copy(slots, slots, sem).wait()

    xbuf[x] = packed
    for peer in x_peers:
        send(xbuf, x, peer, 0)
    arrived(xbuf, 0, NX - 1, recv_sem.at[0])
    zbuf[z] = (xbuf[0] + xbuf[1]) + (xbuf[2] + xbuf[3])
    for peer in z_peers:
        send(zbuf, z, peer, 1)
    arrived(zbuf, 0, NZ - 1, recv_sem.at[1])
    tbuf[tm] = ((zbuf[0] + zbuf[1]) + (zbuf[2] + zbuf[3])) + (
        (zbuf[4] + zbuf[5]) + (zbuf[6] + zbuf[7])
    )
    send(tbuf, tm, sibling, 2)
    for k in range(1, GROUPS):
        for c in range(2):
            send(tbuf, tm, (space, 2 * chips[GROUPS - k] + c), 2 + k)

    half_lane = lax.broadcasted_iota(jnp.int32, (HALF, 128), 1) < 64
    first_row = tm * OWN

    def build(k, count):
        for g in range(k, k + count):
            a, b = tbuf[2 * chips[g]], tbuf[2 * chips[g] + 1]
            modes[g, 0:HALF] = jnp.where(half_lane, a, pltpu.roll(b, 64, 1))
            modes[g, HALF:R] = jnp.where(half_lane, pltpu.roll(a, 64, 1), b)
        part = slice(k, k + count)
        feat[part, 1 : 1 + R] = modes[part, :R]
        for i, at in enumerate(quadratic_rows()):
            rows = -(-(R - i) // 8) * 8
            feat[part, at : at + rows] = modes[part, i : i + rows] * modes[part, i : i + 1]
        feat[part, F:RATE_ROW] = jnp.zeros((count, RATE_ROW - F, 128), jnp.float32)
        for g in range(k, k + count):
            lanes = slice(g * 128, (g + 1) * 128)
            own_ref[0:PAD, lanes], own_ref[PAD : 2 * PAD, lanes] = split(feat[g, pl.ds(first_row, PAD)])

            def step(r, carry, g=g, lanes=lanes):
                at = pl.ds(pl.multiple_of(r * 64, 64), 64)
                hi_ref[at, lanes], lo_ref[at, lanes] = split(feat[g, at])
                return carry

            lax.fori_loop(0, RATE_ROW // 64, step, 0, unroll=4)

    arrived(tbuf, sibling[1], 1, recv_sem.at[2])
    build(0, 1)
    arrived(tbuf, 2 * chips[1], 2, recv_sem.at[3])
    build(1, 1)
    for n in range(EARLY // 256):
        cols = slice(n * 256, (n + 1) * 256)
        part_ref[:, cols] = products(own_ref[:, :256], hi_ref[cols, :256], lo_ref[cols, :256])
    arrived(tbuf, 2 * chips[2], 2, recv_sem.at[4])
    arrived(tbuf, 2 * chips[3], 2, recv_sem.at[5])
    build(2, 2)

    snaps = GROUPS * 128
    whole = jnp.concatenate([modes[g, :72] for g in range(GROUPS)], axis=1)
    when = lax.rem(lax.broadcasted_iota(jnp.int32, (72, snaps), 1) + y * 128, snaps)
    first, last = when == 0, when == snaps - 1
    after = jnp.where(last, whole, pltpu.roll(whole, snaps - 1, 1))
    before = jnp.where(first, whole, pltpu.roll(whole, 1, 1))
    rate = (after - before) * jnp.where(first | last, 1.0, 0.5)
    rate = jnp.concatenate([rate, jnp.zeros((ROWS - RATE_ROW - 72, snaps), jnp.float32)], axis=0)
    hi_ref[RATE_ROW:ROWS], lo_ref[RATE_ROW:ROWS] = split(rate)

    at = core * 64 + 2 * space
    turned[0] = jnp.concatenate([modes[0], jnp.zeros((48, 128), jnp.float32)], axis=0).T
    turned[1] = rate[:, :128].T
    mine_ref[0] = turned[0, pl.ds(at, 2)]
    mine_ref[1] = turned[1, pl.ds(at, 2)]

    for phase, (buf, count) in enumerate(((xbuf, NX - 1), (zbuf, NZ - 1), (tbuf, NT - 1))):
        arrived(buf, 0, count, send_sem.at[phase])


def normal_equations(
    part_ref, own_ref, hi_ref, lo_ref, mine_ref, pen_ref, normal_ref, rhs_ref, state_ref, rate_ref, obuf, rbuf, sem
):
    first_row = lax.axis_index("tm") * OWN
    state_ref[0] = mine_ref[0, :, :R]
    rate_ref[0] = mine_ref[1, :, :R]
    row = lax.broadcasted_iota(jnp.int32, (OWN, 256), 0) + first_row
    col = lax.broadcasted_iota(jnp.int32, (OWN, 256), 1)
    scale = 1.0 / (GROUPS * 128)
    copies = []
    for n in range(ROWS // 256):
        at = slice(n * 256, (n + 1) * 256)
        if n * 256 < EARLY:
            cols, late = at, slice(256, 512)
            gram = products(own_ref[:, late], hi_ref[at, late], lo_ref[at, late]) + part_ref[:, at]
        else:
            cols = slice(n * 256, F)
            gram = products(own_ref[...], hi_ref[at], lo_ref[at])
            rbuf[...] = (gram[:OWN, 128:256] * scale).T[:R]
            gram, row, col = gram[:, : F - n * 256], row[:, : F - n * 256], col[:, : F - n * 256]
        penalty = pen_ref[cols][None, :]
        obuf[:, cols] = gram[:OWN] * scale + jnp.where(row == col + n * 256, penalty, 0.0)
        copies.append(pltpu.make_async_copy(obuf.at[:, cols], normal_ref.at[:, cols], sem.at[n]))
        copies[-1].start()
    copies.append(pltpu.make_async_copy(rbuf, rhs_ref, sem.at[ROWS // 256]))
    copies[-1].start()
    for copy in copies:
        copy.wait()


def shards(snapshots, pod_basis, penalty):
    group, dofs = snapshots.shape
    snaps = GROUPS * 128
    hbm = pl.BlockSpec(memory_space=pltpu.HBM)
    vmem = pl.BlockSpec(memory_space=pltpu.VMEM)
    shared = pl.pallas_call(
        project_and_share,
        out_shape=[
            pltpu.VMEM((PAD, EARLY), jnp.float32),
            pltpu.VMEM((2 * PAD, snaps), jnp.bfloat16),
            pltpu.VMEM((ROWS, snaps), jnp.bfloat16),
            pltpu.VMEM((ROWS, snaps), jnp.bfloat16),
            pltpu.VMEM((2, 2, 128), jnp.float32),
        ],
        in_specs=[hbm, hbm],
        out_specs=[vmem] * 5,
        scratch_shapes=[
            pltpu.VMEM((group, dofs), jnp.bfloat16),
            pltpu.VMEM((R, dofs), jnp.bfloat16),
            pltpu.VMEM((NX, HALF, 128), jnp.float32),
            pltpu.VMEM((NZ, HALF, 128), jnp.float32),
            pltpu.VMEM((NT, HALF, 128), jnp.float32),
            pltpu.VMEM((GROUPS, 80, 128), jnp.float32),
            pltpu.VMEM((GROUPS, RATE_ROW + 16, 128), jnp.float32),
            pltpu.VMEM((2, 128, 128), jnp.float32),
            pltpu.SemaphoreType.DMA((2, CHUNKS)),
            pltpu.SemaphoreType.DMA((3,)),
            pltpu.SemaphoreType.DMA((6,)),
        ],
        compiler_params=pltpu.CompilerParams(
            collective_id=0, has_side_effects=True, vmem_limit_bytes=50 << 20
        ),
        name="project_and_share",
    )(snapshots, pod_basis)
    normal, rhs, state, rates = pl.pallas_call(
        normal_equations,
        out_shape=[
            jax.ShapeDtypeStruct((OWN, F), jnp.float32),
            jax.ShapeDtypeStruct((R, OWN), jnp.float32),
            jax.ShapeDtypeStruct((1, 2, R), jnp.float32),
            jax.ShapeDtypeStruct((1, 2, R), jnp.float32),
        ],
        in_specs=[vmem] * 6,
        out_specs=[hbm, hbm, vmem, vmem],
        scratch_shapes=[
            pltpu.VMEM((OWN, F), jnp.float32),
            pltpu.VMEM((R, OWN), jnp.float32),
            pltpu.SemaphoreType.DMA((ROWS // 256 + 1,)),
        ],
        compiler_params=pltpu.CompilerParams(vmem_limit_bytes=16 << 20),
        name="normal_equations",
    )(*shared, penalty)
    return normal, rhs.T, state, rates


def solution(mesh):
    return jax.shard_map(
        shards,
        mesh=mesh,
        in_specs=(P("tm", "space"), P(None, "space"), P()),
        out_specs=(P("tm", None), P("tm", None), P("tm", "space", None), P("tm", "space", None)),
        check_vma=False,
    )
```

```python
import functools

import jax
import jax.numpy as jnp
from jax import lax
from jax.experimental import pallas as pl
from jax.experimental.pallas import tpu as pltpu
from jax.sharding import PartitionSpec as P

R = 68
HALF = R // 2
F = 1 + R + R * (R + 1) // 2
OWN = (F + 1) // 8
PAD = -(-OWN // 16) * 16
GROUPS = 4
NX, NZ, NT = 4, 8, 8
CHUNKS = (2048, 6144, 6144, 6144, 4096, 4096, 2048, 1024, 1024)
SLOTS = (0, 1, 3, 2)
LAST = 2432
MESH = pl.DeviceIdType.MESH
CONTRACT_LANES = (((1,), (1,)), ((), ()))


def quadratic_rows():
    starts, at = [], 1 + R
    for i in range(R):
        starts.append(at)
        at += R - i
    return starts


def split(value):
    high = value.astype(jnp.bfloat16)
    return high, (value - high.astype(jnp.float32)).astype(jnp.bfloat16)


def dot(a, b):
    return lax.dot_general(a, b, CONTRACT_LANES, preferred_element_type=jnp.float32)


def tiles():
    return [(at, min(at + 256, LAST)) for at in range(0, LAST, 256)]


def pair_products(own, hi, lo):
    both = dot(own, hi)
    return both[:PAD] + both[PAD:] + dot(own[:PAD], lo)


def single_products(own, hi, lo):
    high = own[:PAD]
    whole = dot(jnp.concatenate([high, high], axis=1), jnp.concatenate([hi, lo], axis=1))
    return whole + dot(own[PAD:], hi)


def project_and_share(
    snap_hbm, pod_hbm, part_ref, own_ref, late_ref, modes,
    snap, pod, xbuf, zbuf, tbuf, feat, load_sem, send_sem, recv_sem
):
    space, tm = lax.axis_index("space"), lax.axis_index("tm")
    z, x = space // NX, lax.rem(space, NX)
    y, core = tm // 2, lax.rem(tm, 2)
    x_peers = [(z * NX + lax.rem(x + k, NX), tm) for k in (2, 1, 3)]
    z_peers = [(lax.rem(z + k, NZ) * NX + x, tm) for k in (4, 3, 5, 2, 6, 1, 7)]
    chips = [lax.rem(y + k, GROUPS) for k in range(GROUPS)]
    sibling = (space, 2 * y + (1 - core))
    t_peers = [sibling] + [(space, 2 * chips[k] + c) for k in range(1, GROUPS) for c in range(2)]

    loads, at = [], 0
    for i, width in enumerate(CHUNKS):
        cols = slice(at, at + width)
        at += width
        loads.append((
            cols,
            pltpu.make_async_copy(snap_hbm.at[:, cols], snap.at[:, cols], load_sem.at[0, i]),
            pltpu.make_async_copy(pod_hbm.at[:, cols], pod.at[:, cols], load_sem.at[1, i]),
        ))
    for _, first, second in loads:
        first.start()
        second.start()

    barrier = pltpu.get_barrier_semaphore()
    peers = z_peers + t_peers + x_peers
    for peer in peers:
        pl.semaphore_signal(barrier, inc=1, device_id=peer, device_id_type=MESH)

    for g in range(GROUPS):
        place(feat, late_ref, g, slice(0, 1), jnp.ones((1, 128), jnp.float32))
    modes[:, R:80] = jnp.zeros((GROUPS, 80 - R, 128), jnp.float32)

    total = jnp.zeros((R, snap_hbm.shape[0]), jnp.float32)
    for cols, first, second in loads:
        first.wait()
        second.wait()
        total = total + dot(pod[:, cols], snap[:, cols])
    packed = jnp.concatenate([total[:HALF], total[HALF:]], axis=1)

    pl.semaphore_wait(barrier, len(peers))

    def send(buf, rank, peer, phase):
        pltpu.make_async_remote_copy(
            src_ref=buf.at[rank],
            dst_ref=buf.at[rank],
            send_sem=send_sem.at[min(phase, 2)],
            recv_sem=recv_sem.at[phase],
            device_id=peer,
            device_id_type=MESH,
        ).start()

    def arrived(buf, at, count, sem):
        slots = buf.at[pl.ds(at, count)]
        pltpu.make_async_copy(slots, slots, sem).wait()

    xbuf[x] = packed
    for peer in x_peers:
        send(xbuf, x, peer, 0)
    arrived(xbuf, 0, NX - 1, recv_sem.at[0])
    zbuf[z] = (xbuf[0] + xbuf[1]) + (xbuf[2] + xbuf[3])
    for peer in z_peers:
        send(zbuf, z, peer, 1)
    arrived(zbuf, 0, NZ - 1, recv_sem.at[1])
    tbuf[tm] = ((zbuf[0] + zbuf[1]) + (zbuf[2] + zbuf[3])) + (
        (zbuf[4] + zbuf[5]) + (zbuf[6] + zbuf[7])
    )
    send(tbuf, tm, sibling, 2)
    for k in SLOTS[1:]:
        for c in range(2):
            send(tbuf, tm, (space, 2 * chips[GROUPS - k] + c), 2 + k)

    half_lane = lax.broadcasted_iota(jnp.int32, (HALF, 128), 1) < 64
    first_row = tm * OWN

    def build(g):
        chip = chips[SLOTS[g]]
        a, b = tbuf[2 * chip], tbuf[2 * chip + 1]
        modes[g, 0:HALF] = jnp.where(half_lane, a, pltpu.roll(b, 64, 1))
        modes[g, HALF:R] = jnp.where(half_lane, pltpu.roll(a, 64, 1), b)
        place(feat, late_ref, g, slice(1, 1 + R), modes[g, :R])
        for i, at in enumerate(quadratic_rows()):
            rows = -(-(R - i) // 8) * 8
            place(feat, late_ref, g, slice(at, at + rows), modes[g, i : i + rows] * modes[g, i : i + 1])
        place(feat, late_ref, g, slice(F, LAST), jnp.zeros((LAST - F, 128), jnp.float32))
        mine = pl.ds(first_row, PAD)
        value = late_ref[mine] if g == GROUPS - 1 else feat[g, mine]
        lanes = slice(g * 128, (g + 1) * 128)
        own_ref[0:PAD, lanes], own_ref[PAD : 2 * PAD, lanes] = split(value)

    arrived(tbuf, sibling[1], 1, recv_sem.at[2])
    build(0)
    own = own_ref[:, 0:128]
    for at, end in tiles():
        part_ref[:, at:end] = single_products(own, *split(feat[0, at:end]))
    arrived(tbuf, 2 * chips[1], 2, recv_sem.at[3])
    build(1)
    arrived(tbuf, 2 * chips[3], 2, recv_sem.at[5])
    build(2)
    own = own_ref[:, 128:384]
    for at, end in tiles():
        value = jnp.concatenate([feat[1, at:end], feat[2, at:end]], axis=1)
        part_ref[:, at:end] += pair_products(own, *split(value))
    arrived(tbuf, 2 * chips[2], 2, recv_sem.at[4])
    build(3)

    for phase, (buf, count) in enumerate(((xbuf, NX - 1), (zbuf, NZ - 1), (tbuf, NT - 1))):
        arrived(buf, 0, count, send_sem.at[phase])


def place(feat, late_ref, g, rows, value):
    if g == GROUPS - 1:
        late_ref[rows] = value
    else:
        feat[g, rows] = value


def normal_equations(
    part_ref, own_ref, late_ref, modes, pen_ref, normal_ref, rhs_ref, state_ref, rate_ref, turned, obuf, rbuf, sem
):
    space, tm = lax.axis_index("space"), lax.axis_index("tm")
    first_row = tm * OWN
    snaps = GROUPS * 128
    scale = 1.0 / snaps
    own = own_ref[:, (GROUPS - 1) * 128 :]
    copies = []
    for n, (at, end) in enumerate(tiles()):
        cols = slice(at, min(end, F))
        width = cols.stop - at
        gram = single_products(own, *split(late_ref[at:end])) + part_ref[:, at:end]
        row = lax.broadcasted_iota(jnp.int32, (OWN, width), 0) + first_row
        col = lax.broadcasted_iota(jnp.int32, (OWN, width), 1) + at
        obuf[:, cols] = gram[:OWN, :width] * scale + jnp.where(row == col, pen_ref[cols][None, :], 0.0)
        copies.append(pltpu.make_async_copy(obuf.at[:, cols], normal_ref.at[:, cols], sem.at[n]))
        copies[-1].start()

        if n == 2:
            order = [modes[SLOTS.index(k), :72] for k in range(GROUPS)]
            whole = jnp.concatenate(order, axis=1)
            when = lax.rem(lax.broadcasted_iota(jnp.int32, (72, snaps), 1) + (tm // 2) * 128, snaps)
            first, last = when == 0, when == snaps - 1
            after = jnp.where(last, whole, pltpu.roll(whole, snaps - 1, 1))
            before = jnp.where(first, whole, pltpu.roll(whole, 1, 1))
            rate = (after - before) * jnp.where(first | last, 1.0, 0.5)
            rate = jnp.concatenate([rate, jnp.zeros((56, snaps), jnp.float32)], axis=0)
            turned[0] = jnp.concatenate([whole[:, :128], jnp.zeros((56, 128), jnp.float32)], axis=0).T
            turned[1] = rate[:, :128].T
            mine = lax.rem(tm, 2) * 64 + 2 * space
            state_ref[0] = turned[0, pl.ds(mine, 2)][:, :R]
            rate_ref[0] = turned[1, pl.ds(mine, 2)][:, :R]
            rate = jnp.concatenate([rate[:, 128 * k : 128 * (k + 1)] for k in SLOTS], axis=1)
            rhs = pair_products(own_ref[...], *split(rate))
            rbuf[...] = (rhs[:OWN] * scale).T[:R]
            copies.append(pltpu.make_async_copy(rbuf, rhs_ref, sem.at[len(tiles())]))
            copies[-1].start()
    for copy in copies:
        copy.wait()


def shards(snapshots, pod_basis, penalty):
    group, dofs = snapshots.shape
    snaps = GROUPS * 128
    hbm = pl.BlockSpec(memory_space=pltpu.HBM)
    vmem = pl.BlockSpec(memory_space=pltpu.VMEM)
    shared = pl.pallas_call(
        project_and_share,
        out_shape=[
            pltpu.VMEM((PAD, LAST), jnp.float32),
            pltpu.VMEM((2 * PAD, snaps), jnp.bfloat16),
            pltpu.VMEM((LAST, 128), jnp.float32),
            pltpu.VMEM((GROUPS, 80, 128), jnp.float32),
        ],
        in_specs=[hbm, hbm],
        out_specs=[vmem] * 4,
        scratch_shapes=[
            pltpu.VMEM((group, dofs), jnp.bfloat16),
            pltpu.VMEM((R, dofs), jnp.bfloat16),
            pltpu.VMEM((NX, HALF, 128), jnp.float32),
            pltpu.VMEM((NZ, HALF, 128), jnp.float32),
            pltpu.VMEM((NT, HALF, 128), jnp.float32),
            pltpu.VMEM((GROUPS - 1, LAST, 128), jnp.float32),
            pltpu.SemaphoreType.DMA((2, len(CHUNKS))),
            pltpu.SemaphoreType.DMA((3,)),
            pltpu.SemaphoreType.DMA((6,)),
        ],
        compiler_params=pltpu.CompilerParams(
            collective_id=0, has_side_effects=True, vmem_limit_bytes=54 << 20
        ),
        name="project_and_share",
    )(snapshots, pod_basis)
    normal, rhs, state, rates = pl.pallas_call(
        normal_equations,
        out_shape=[
            jax.ShapeDtypeStruct((OWN, F), jnp.float32),
            jax.ShapeDtypeStruct((R, OWN), jnp.float32),
            jax.ShapeDtypeStruct((1, 2, R), jnp.float32),
            jax.ShapeDtypeStruct((1, 2, R), jnp.float32),
        ],
        in_specs=[vmem] * 5,
        out_specs=[hbm, hbm, vmem, vmem],
        scratch_shapes=[
            pltpu.VMEM((2, 128, 128), jnp.float32),
            pltpu.VMEM((OWN, F), jnp.float32),
            pltpu.VMEM((R, OWN), jnp.float32),
            pltpu.SemaphoreType.DMA((len(tiles()) + 1,)),
        ],
        compiler_params=pltpu.CompilerParams(vmem_limit_bytes=16 << 20),
        name="normal_equations",
    )(*shared, penalty)
    return normal, rhs.T, state, rates


def solution(mesh):
    return jax.shard_map(
        shards,
        mesh=mesh,
        in_specs=(P("tm", "space"), P(None, "space"), P()),
        out_specs=(P("tm", None), P("tm", None), P("tm", "space", None), P("tm", "space", None)),
        check_vma=False,
    )
```

```python
import functools

import jax
import jax.numpy as jnp
from jax import lax
from jax.experimental import pallas as pl
from jax.experimental.pallas import tpu as pltpu
from jax.sharding import PartitionSpec as P

R = 68
HALF = R // 2
F = 1 + R + R * (R + 1) // 2
OWN = (F + 1) // 8
PAD = -(-OWN // 16) * 16
GROUPS = 4
NX, NZ, NT = 4, 8, 8
CHUNKS = (2048, 6144, 6144, 6144, 4096, 4096, 2048, 1024, 1024)
SLOTS = (0, 1, 3, 2)
LAST = 2432
MESH = pl.DeviceIdType.MESH
CONTRACT_LANES = (((1,), (1,)), ((), ()))


def quadratic_rows():
    starts, at = [], 1 + R
    for i in range(R):
        starts.append(at)
        at += R - i
    return starts


def split(value):
    high = value.astype(jnp.bfloat16)
    return high, (value - high.astype(jnp.float32)).astype(jnp.bfloat16)


def dot(a, b):
    return lax.dot_general(a, b, CONTRACT_LANES, preferred_element_type=jnp.float32)


def tiles():
    return [(at, min(at + 256, LAST)) for at in range(0, LAST, 256)]


def pair_products(own, hi, lo):
    both = dot(own, hi)
    return both[:PAD] + both[PAD:] + dot(own[:PAD], lo)


def single_products(own, hi, lo):
    high = own[:PAD]
    whole = dot(jnp.concatenate([high, high], axis=1), jnp.concatenate([hi, lo], axis=1))
    return whole + dot(own[PAD:], hi)


def project_and_share(
    snap_hbm, pod_hbm, pen_hbm, part_ref, own_ref, late_ref, modes,
    snap, pod, pen, xbuf, zbuf, tbuf, feat, load_sem, pen_sem, send_sem, recv_sem
):
    space, tm = lax.axis_index("space"), lax.axis_index("tm")
    z, x = space // NX, lax.rem(space, NX)
    y, core = tm // 2, lax.rem(tm, 2)
    x_peers = [(z * NX + lax.rem(x + k, NX), tm) for k in (2, 1, 3)]
    z_peers = [(lax.rem(z + k, NZ) * NX + x, tm) for k in (4, 3, 5, 2, 6, 1, 7)]
    chips = [lax.rem(y + k, GROUPS) for k in range(GROUPS)]
    sibling = (space, 2 * y + (1 - core))
    t_peers = [sibling] + [(space, 2 * chips[k] + c) for k in range(1, GROUPS) for c in range(2)]

    loads, at = [], 0
    for i, width in enumerate(CHUNKS):
        cols = slice(at, at + width)
        at += width
        loads.append((
            cols,
            pltpu.make_async_copy(snap_hbm.at[:, cols], snap.at[:, cols], load_sem.at[0, i]),
            pltpu.make_async_copy(pod_hbm.at[:, cols], pod.at[:, cols], load_sem.at[1, i]),
        ))
    for _, first, second in loads:
        first.start()
        second.start()
    pen_copy = pltpu.make_async_copy(pen_hbm, pen, pen_sem)
    pen_copy.start()

    barrier = pltpu.get_barrier_semaphore()
    peers = z_peers + t_peers + x_peers
    for peer in peers:
        pl.semaphore_signal(barrier, inc=1, device_id=peer, device_id_type=MESH)

    for g in range(GROUPS):
        place(feat, late_ref, g, slice(0, 1), jnp.ones((1, 128), jnp.float32))
    modes[:, R:80] = jnp.zeros((GROUPS, 80 - R, 128), jnp.float32)

    total = jnp.zeros((R, snap_hbm.shape[0]), jnp.float32)
    for cols, first, second in loads:
        first.wait()
        second.wait()
        total = total + dot(pod[:, cols], snap[:, cols])
    packed = jnp.concatenate([total[:HALF], total[HALF:]], axis=1)

    pl.semaphore_wait(barrier, len(peers))

    def send(buf, rank, peer, phase):
        pltpu.make_async_remote_copy(
            src_ref=buf.at[rank],
            dst_ref=buf.at[rank],
            send_sem=send_sem.at[min(phase, 2)],
            recv_sem=recv_sem.at[phase],
            device_id=peer,
            device_id_type=MESH,
        ).start()

    def arrived(buf, at, count, sem):
        slots = buf.at[pl.ds(at, count)]
        pltpu.make_async_copy(slots, slots, sem).wait()

    xbuf[x] = packed
    for peer in x_peers:
        send(xbuf, x, peer, 0)
    arrived(xbuf, 0, NX - 1, recv_sem.at[0])
    zbuf[z] = (xbuf[0] + xbuf[1]) + (xbuf[2] + xbuf[3])
    for peer in z_peers:
        send(zbuf, z, peer, 1)
    arrived(zbuf, 0, NZ - 1, recv_sem.at[1])
    tbuf[tm] = ((zbuf[0] + zbuf[1]) + (zbuf[2] + zbuf[3])) + (
        (zbuf[4] + zbuf[5]) + (zbuf[6] + zbuf[7])
    )
    send(tbuf, tm, sibling, 2)
    for k in SLOTS[1:]:
        for c in range(2):
            send(tbuf, tm, (space, 2 * chips[GROUPS - k] + c), 2 + k)

    half_lane = lax.broadcasted_iota(jnp.int32, (HALF, 128), 1) < 64
    first_row = tm * OWN

    def build(g):
        chip = chips[SLOTS[g]]
        a, b = tbuf[2 * chip], tbuf[2 * chip + 1]
        modes[g, 0:HALF] = jnp.where(half_lane, a, pltpu.roll(b, 64, 1))
        modes[g, HALF:R] = jnp.where(half_lane, pltpu.roll(a, 64, 1), b)
        place(feat, late_ref, g, slice(1, 1 + R), modes[g, :R])
        for i, at in enumerate(quadratic_rows()):
            rows = -(-(R - i) // 8) * 8
            place(feat, late_ref, g, slice(at, at + rows), modes[g, i : i + rows] * modes[g, i : i + 1])
        place(feat, late_ref, g, slice(F, LAST), jnp.zeros((LAST - F, 128), jnp.float32))
        mine = pl.ds(first_row, PAD)
        value = (feat[g, mine] if g < 2 else late_ref[g - 2, mine]) * (1.0 / (GROUPS * 128))
        lanes = slice(g * 128, (g + 1) * 128)
        own_ref[0:PAD, lanes], own_ref[PAD : 2 * PAD, lanes] = split(value)

    arrived(tbuf, sibling[1], 1, recv_sem.at[2])
    build(0)
    pen_copy.wait()
    own = own_ref[:, 0:128]
    for at, end in tiles():
        penalty = pen[at : min(end, F)][None, :]
        if end > F:
            penalty = jnp.concatenate([penalty, jnp.zeros((1, end - F), jnp.float32)], axis=1)
        row = lax.broadcasted_iota(jnp.int32, (PAD, end - at), 0) + first_row
        col = lax.broadcasted_iota(jnp.int32, (PAD, end - at), 1) + at
        diagonal = jnp.where(row == col, penalty, 0.0)
        part_ref[:, at:end] = single_products(own, *split(feat[0, at:end])) + diagonal
    arrived(tbuf, 2 * chips[1], 2, recv_sem.at[3])
    build(1)
    own = own_ref[:, 128:256]
    for at, end in tiles():
        part_ref[:, at:end] += single_products(own, *split(feat[1, at:end]))
    arrived(tbuf, 2 * chips[3], 2, recv_sem.at[5])
    build(2)
    arrived(tbuf, 2 * chips[2], 2, recv_sem.at[4])
    build(3)

    for phase, (buf, count) in enumerate(((xbuf, NX - 1), (zbuf, NZ - 1), (tbuf, NT - 1))):
        arrived(buf, 0, count, send_sem.at[phase])


def place(feat, late_ref, g, rows, value):
    if g < 2:
        feat[g, rows] = value
    else:
        late_ref[g - 2, rows] = value


def normal_equations(
    part_ref, own_ref, late_ref, modes, normal_ref, rhs_ref, state_ref, rate_ref, turned, obuf, rbuf, mine, sem
):
    space, tm = lax.axis_index("space"), lax.axis_index("tm")
    snaps = GROUPS * 128
    own = own_ref[:, snaps // 2 :]
    copies = []

    def write(source, target, n):
        copies.append(pltpu.make_async_copy(source, target, sem.at[n]))
        copies[-1].start()

    for n, (at, end) in enumerate(tiles()):
        cols = slice(at, min(end, F))
        value = jnp.concatenate([late_ref[0, at:end], late_ref[1, at:end]], axis=1)
        gram = pair_products(own, *split(value)) + part_ref[:, at:end]
        obuf[:, cols] = gram[:OWN, : cols.stop - at]
        write(obuf.at[:, cols], normal_ref.at[:, cols], n)

        if n == 6:
            order = [modes[SLOTS.index(k), :72] for k in range(GROUPS)]
            whole = jnp.concatenate(order, axis=1)
            when = lax.rem(lax.broadcasted_iota(jnp.int32, (72, snaps), 1) + (tm // 2) * 128, snaps)
            first, last = when == 0, when == snaps - 1
            after = jnp.where(last, whole, pltpu.roll(whole, snaps - 1, 1))
            before = jnp.where(first, whole, pltpu.roll(whole, 1, 1))
            rate = (after - before) * jnp.where(first | last, 1.0, 0.5)
            rate = jnp.concatenate([rate, jnp.zeros((56, snaps), jnp.float32)], axis=0)
            turned[0] = jnp.concatenate([whole[:, :128], jnp.zeros((56, 128), jnp.float32)], axis=0).T
            turned[1] = rate[:, :128].T
            here = lax.rem(tm, 2) * 64 + 2 * space
            mine[0, 0] = turned[0, pl.ds(here, 2)][:, :R]
            mine[1, 0] = turned[1, pl.ds(here, 2)][:, :R]
            write(mine.at[0], state_ref, len(tiles()) + 1)
            write(mine.at[1], rate_ref, len(tiles()) + 2)
            rate = jnp.concatenate([rate[:, 128 * k : 128 * (k + 1)] for k in SLOTS], axis=1)
            rhs = pair_products(own_ref[...], *split(rate))
            rbuf[...] = rhs[:OWN].T[:R]
            write(rbuf, rhs_ref, len(tiles()))
    for copy in copies:
        copy.wait()


def shards(snapshots, pod_basis, penalty):
    group, dofs = snapshots.shape
    snaps = GROUPS * 128
    hbm = pl.BlockSpec(memory_space=pltpu.HBM)
    vmem = pl.BlockSpec(memory_space=pltpu.VMEM)
    shared = pl.pallas_call(
        project_and_share,
        out_shape=[
            pltpu.VMEM((PAD, LAST), jnp.float32),
            pltpu.VMEM((2 * PAD, snaps), jnp.bfloat16),
            pltpu.VMEM((2, LAST, 128), jnp.float32),
            pltpu.VMEM((GROUPS, 80, 128), jnp.float32),
        ],
        in_specs=[hbm, hbm, hbm],
        out_specs=[vmem] * 4,
        scratch_shapes=[
            pltpu.VMEM((group, dofs), jnp.bfloat16),
            pltpu.VMEM((R, dofs), jnp.bfloat16),
            pltpu.VMEM((F,), jnp.float32),
            pltpu.VMEM((NX, HALF, 128), jnp.float32),
            pltpu.VMEM((NZ, HALF, 128), jnp.float32),
            pltpu.VMEM((NT, HALF, 128), jnp.float32),
            pltpu.VMEM((2, LAST, 128), jnp.float32),
            pltpu.SemaphoreType.DMA((2, len(CHUNKS))),
            pltpu.SemaphoreType.DMA,
            pltpu.SemaphoreType.DMA((3,)),
            pltpu.SemaphoreType.DMA((6,)),
        ],
        compiler_params=pltpu.CompilerParams(
            collective_id=0, has_side_effects=True, vmem_limit_bytes=53 << 20
        ),
        name="project_and_share",
    )(snapshots, pod_basis, penalty)
    normal, rhs, state, rates = pl.pallas_call(
        normal_equations,
        out_shape=[
            jax.ShapeDtypeStruct((OWN, F), jnp.float32),
            jax.ShapeDtypeStruct((R, OWN), jnp.float32),
            jax.ShapeDtypeStruct((1, 2, R), jnp.float32),
            jax.ShapeDtypeStruct((1, 2, R), jnp.float32),
        ],
        in_specs=[vmem] * 4,
        out_specs=[hbm] * 4,
        scratch_shapes=[
            pltpu.VMEM((2, 128, 128), jnp.float32),
            pltpu.VMEM((OWN, F), jnp.float32),
            pltpu.VMEM((R, OWN), jnp.float32),
            pltpu.VMEM((2, 1, 2, R), jnp.float32),
            pltpu.SemaphoreType.DMA((len(tiles()) + 3,)),
        ],
        compiler_params=pltpu.CompilerParams(vmem_limit_bytes=16 << 20),
        name="normal_equations",
    )(*shared)
    return normal, rhs.T, state, rates


def solution(mesh):
    return jax.shard_map(
        shards,
        mesh=mesh,
        in_specs=(P("tm", "space"), P(None, "space"), P()),
        out_specs=(P("tm", None), P("tm", None), P("tm", "space", None), P("tm", "space", None)),
        check_vma=False,
    )
```

```python
import functools

import jax
import jax.numpy as jnp
from jax import lax
from jax.experimental import pallas as pl
from jax.experimental.pallas import tpu as pltpu
from jax.sharding import PartitionSpec as P

R = 68
HALF = R // 2
F = 1 + R + R * (R + 1) // 2
OWN = (F + 1) // 8
PAD = -(-OWN // 16) * 16
GROUPS = 4
NX, NZ, NT = 4, 8, 8
CHUNKS = (1024, 2048) + (3072,) * 9 + (1024, 512, 512)
SLOTS = (0, 1, 3, 2)
LAST = 2432
MESH = pl.DeviceIdType.MESH
CONTRACT_LANES = (((1,), (1,)), ((), ()))


def quadratic_rows():
    starts, at = [], 1 + R
    for i in range(R):
        starts.append(at)
        at += R - i
    return starts


def split(value):
    high = value.astype(jnp.bfloat16)
    return high, (value - high.astype(jnp.float32)).astype(jnp.bfloat16)


def dot(a, b):
    return lax.dot_general(a, b, CONTRACT_LANES, preferred_element_type=jnp.float32)


def tiles():
    return [(at, min(at + 256, LAST)) for at in range(0, LAST, 256)]


def pair_products(own, hi, lo):
    both = dot(own, hi)
    return both[:PAD] + both[PAD:] + dot(own[:PAD], lo)


def single_products(own, hi, lo):
    high = own[:PAD]
    whole = dot(jnp.concatenate([high, high], axis=1), jnp.concatenate([hi, lo], axis=1))
    return whole + dot(own[PAD:], hi)


def project_and_share(
    snap_hbm, pod_hbm, pen_hbm, part_ref, own_ref, late_ref, modes,
    snap, pod, pen, xbuf, zbuf, tbuf, feat, load_sem, pen_sem, send_sem, recv_sem
):
    space, tm = lax.axis_index("space"), lax.axis_index("tm")
    z, x = space // NX, lax.rem(space, NX)
    y, core = tm // 2, lax.rem(tm, 2)
    x_peers = [(z * NX + k + (x <= k).astype(jnp.int32), tm) for k in range(NX - 1)]
    z_peers = [((k + (z <= k).astype(jnp.int32)) * NX + x, tm) for k in range(NZ - 1)]
    chips = [lax.rem(y + k, GROUPS) for k in range(GROUPS)]
    sibling = (space, 2 * y + (1 - core))
    y_peers = [k + (y <= k).astype(jnp.int32) for k in range(GROUPS - 1)]
    t_peers = [sibling] + [(space, 2 * chip + c) for chip in y_peers for c in range(2)]

    loads, at = [], 0
    for i, width in enumerate(CHUNKS):
        cols = slice(at, at + width)
        at += width
        loads.append((
            cols,
            pltpu.make_async_copy(snap_hbm.at[:, cols], snap.at[:, cols], load_sem.at[0, i]),
            pltpu.make_async_copy(pod_hbm.at[:, cols], pod.at[:, cols], load_sem.at[1, i]),
        ))
    for _, first, second in loads:
        first.start()
        second.start()
    pen_copy = pltpu.make_async_copy(pen_hbm, pen, pen_sem)
    pen_copy.start()

    barrier = pltpu.get_barrier_semaphore()
    peers = z_peers + t_peers + x_peers
    for peer in peers:
        pl.semaphore_signal(barrier, inc=1, device_id=peer, device_id_type=MESH)

    for g in range(GROUPS):
        place(feat, late_ref, g, slice(0, 1), jnp.ones((1, 128), jnp.float32))
    modes[:, R:80] = jnp.zeros((GROUPS, 80 - R, 128), jnp.float32)

    total = jnp.zeros((R, snap_hbm.shape[0]), jnp.float32)
    for cols, first, second in loads:
        first.wait()
        second.wait()
        total = total + dot(pod[:, cols], snap[:, cols])
    packed = jnp.concatenate([total[:HALF], total[HALF:]], axis=1)

    pl.semaphore_wait(barrier, len(peers))

    def send(buf, rank, peer, way, phase):
        pltpu.make_async_remote_copy(
            src_ref=buf.at[rank],
            dst_ref=buf.at[rank],
            send_sem=send_sem.at[way],
            recv_sem=recv_sem.at[phase],
            device_id=peer,
            device_id_type=MESH,
        ).start()

    def arrived(buf, at, count, sem):
        slots = buf.at[pl.ds(at, count)]
        pltpu.make_async_copy(slots, slots, sem).wait()

    xbuf[x] = packed
    for peer in x_peers:
        send(xbuf, x, peer, 0, 0)
    arrived(xbuf, 0, NX - 1, recv_sem.at[0])
    zbuf[z] = (xbuf[0] + xbuf[1]) + (xbuf[2] + xbuf[3])
    for peer in z_peers:
        send(zbuf, z, peer, 1, 1)
    arrived(zbuf, 0, NZ - 1, recv_sem.at[1])
    tbuf[tm] = ((zbuf[0] + zbuf[1]) + (zbuf[2] + zbuf[3])) + (
        (zbuf[4] + zbuf[5]) + (zbuf[6] + zbuf[7])
    )
    send(tbuf, tm, sibling, 2, 2)
    for chip in y_peers:
        for c in range(2):
            send(tbuf, tm, (space, 2 * chip + c), 2, 2 + lax.rem(y - chip + GROUPS, GROUPS))

    half_lane = lax.broadcasted_iota(jnp.int32, (HALF, 128), 1) < 64
    first_row = tm * OWN

    def build(g):
        chip = chips[SLOTS[g]]
        a, b = tbuf[2 * chip], tbuf[2 * chip + 1]
        modes[g, 0:HALF] = jnp.where(half_lane, a, pltpu.roll(b, 64, 1))
        modes[g, HALF:R] = jnp.where(half_lane, pltpu.roll(a, 64, 1), b)
        place(feat, late_ref, g, slice(1, 1 + R), modes[g, :R])
        for i, at in enumerate(quadratic_rows()):
            rows = -(-(R - i) // 8) * 8
            place(feat, late_ref, g, slice(at, at + rows), modes[g, i : i + rows] * modes[g, i : i + 1])
        place(feat, late_ref, g, slice(F, LAST), jnp.zeros((LAST - F, 128), jnp.float32))
        mine = pl.ds(first_row, PAD)
        value = (feat[g, mine] if g < 2 else late_ref[g - 2, mine]) * (1.0 / (GROUPS * 128))
        lanes = slice(g * 128, (g + 1) * 128)
        own_ref[0:PAD, lanes], own_ref[PAD : 2 * PAD, lanes] = split(value)

    arrived(tbuf, sibling[1], 1, recv_sem.at[2])
    build(0)
    pen_copy.wait()
    own = own_ref[:, 0:128]
    for at, end in tiles():
        penalty = pen[at : min(end, F)][None, :]
        if end > F:
            penalty = jnp.concatenate([penalty, jnp.zeros((1, end - F), jnp.float32)], axis=1)
        row = lax.broadcasted_iota(jnp.int32, (PAD, end - at), 0) + first_row
        col = lax.broadcasted_iota(jnp.int32, (PAD, end - at), 1) + at
        diagonal = jnp.where(row == col, penalty, 0.0)
        part_ref[:, at:end] = single_products(own, *split(feat[0, at:end])) + diagonal
    arrived(tbuf, 2 * chips[1], 2, recv_sem.at[3])
    build(1)
    own = own_ref[:, 128:256]
    for at, end in tiles():
        part_ref[:, at:end] += single_products(own, *split(feat[1, at:end]))
    arrived(tbuf, 2 * chips[3], 2, recv_sem.at[5])
    build(2)
    arrived(tbuf, 2 * chips[2], 2, recv_sem.at[4])
    build(3)

    for way, buf, count in ((0, xbuf, NX - 1), (1, zbuf, NZ - 1), (2, tbuf, NT - 1)):
        arrived(buf, 0, count, send_sem.at[way])


def place(feat, late_ref, g, rows, value):
    if g < 2:
        feat[g, rows] = value
    else:
        late_ref[g - 2, rows] = value


def normal_equations(
    part_ref, own_ref, late_ref, modes, normal_ref, rhs_ref, state_ref, rate_ref, turned, obuf, rbuf, mine, sem
):
    space, tm = lax.axis_index("space"), lax.axis_index("tm")
    snaps = GROUPS * 128
    own = own_ref[:, snaps // 2 :]
    copies = []

    def write(source, target, n):
        copies.append(pltpu.make_async_copy(source, target, sem.at[n]))
        copies[-1].start()

    for n, (at, end) in enumerate(tiles()):
        cols = slice(at, min(end, F))
        value = jnp.concatenate([late_ref[0, at:end], late_ref[1, at:end]], axis=1)
        gram = pair_products(own, *split(value)) + part_ref[:, at:end]
        obuf[:, cols] = gram[:OWN, : cols.stop - at]
        write(obuf.at[:, cols], normal_ref.at[:, cols], n)

        if n == 6:
            order = [modes[SLOTS.index(k), :72] for k in range(GROUPS)]
            whole = jnp.concatenate(order, axis=1)
            when = lax.rem(lax.broadcasted_iota(jnp.int32, (72, snaps), 1) + (tm // 2) * 128, snaps)
            first, last = when == 0, when == snaps - 1
            after = jnp.where(last, whole, pltpu.roll(whole, snaps - 1, 1))
            before = jnp.where(first, whole, pltpu.roll(whole, 1, 1))
            rate = (after - before) * jnp.where(first | last, 1.0, 0.5)
            rate = jnp.concatenate([rate, jnp.zeros((56, snaps), jnp.float32)], axis=0)
            turned[0] = jnp.concatenate([whole[:, :128], jnp.zeros((56, 128), jnp.float32)], axis=0).T
            turned[1] = rate[:, :128].T
            here = lax.rem(tm, 2) * 64 + 2 * space
            mine[0, 0] = turned[0, pl.ds(here, 2)][:, :R]
            mine[1, 0] = turned[1, pl.ds(here, 2)][:, :R]
            write(mine.at[0], state_ref, len(tiles()) + 1)
            write(mine.at[1], rate_ref, len(tiles()) + 2)
            rate = jnp.concatenate([rate[:, 128 * k : 128 * (k + 1)] for k in SLOTS], axis=1)
            rhs = pair_products(own_ref[...], *split(rate))
            rbuf[...] = rhs[:OWN].T[:R]
            write(rbuf, rhs_ref, len(tiles()))
    for copy in copies:
        copy.wait()


def shards(snapshots, pod_basis, penalty):
    group, dofs = snapshots.shape
    snaps = GROUPS * 128
    hbm = pl.BlockSpec(memory_space=pltpu.HBM)
    vmem = pl.BlockSpec(memory_space=pltpu.VMEM)
    shared = pl.pallas_call(
        project_and_share,
        out_shape=[
            pltpu.VMEM((PAD, LAST), jnp.float32),
            pltpu.VMEM((2 * PAD, snaps), jnp.bfloat16),
            pltpu.VMEM((2, LAST, 128), jnp.float32),
            pltpu.VMEM((GROUPS, 80, 128), jnp.float32),
        ],
        in_specs=[hbm, hbm, hbm],
        out_specs=[vmem] * 4,
        scratch_shapes=[
            pltpu.VMEM((group, dofs), jnp.bfloat16),
            pltpu.VMEM((R, dofs), jnp.bfloat16),
            pltpu.VMEM((F,), jnp.float32),
            pltpu.VMEM((NX, HALF, 128), jnp.float32),
            pltpu.VMEM((NZ, HALF, 128), jnp.float32),
            pltpu.VMEM((NT, HALF, 128), jnp.float32),
            pltpu.VMEM((2, LAST, 128), jnp.float32),
            pltpu.SemaphoreType.DMA((2, len(CHUNKS))),
            pltpu.SemaphoreType.DMA,
            pltpu.SemaphoreType.DMA((3,)),
            pltpu.SemaphoreType.DMA((6,)),
        ],
        compiler_params=pltpu.CompilerParams(
            collective_id=0, has_side_effects=True, vmem_limit_bytes=53 << 20
        ),
        name="project_and_share",
    )(snapshots, pod_basis, penalty)
    normal, rhs, state, rates = pl.pallas_call(
        normal_equations,
        out_shape=[
            jax.ShapeDtypeStruct((OWN, F), jnp.float32),
            jax.ShapeDtypeStruct((R, OWN), jnp.float32),
            jax.ShapeDtypeStruct((1, 2, R), jnp.float32),
            jax.ShapeDtypeStruct((1, 2, R), jnp.float32),
        ],
        in_specs=[vmem] * 4,
        out_specs=[hbm] * 4,
        scratch_shapes=[
            pltpu.VMEM((2, 128, 128), jnp.float32),
            pltpu.VMEM((OWN, F), jnp.float32),
            pltpu.VMEM((R, OWN), jnp.float32),
            pltpu.VMEM((2, 1, 2, R), jnp.float32),
            pltpu.SemaphoreType.DMA((len(tiles()) + 3,)),
        ],
        compiler_params=pltpu.CompilerParams(vmem_limit_bytes=16 << 20),
        name="normal_equations",
    )(*shared)
    return normal, rhs.T, state, rates


def solution(mesh):
    return jax.shard_map(
        shards,
        mesh=mesh,
        in_specs=(P("tm", "space"), P(None, "space"), P()),
        out_specs=(P("tm", None), P("tm", None), P("tm", "space", None), P("tm", "space", None)),
        check_vma=False,
    )
```

```python
import functools

import jax
import jax.numpy as jnp
from jax import lax
from jax.experimental import pallas as pl
from jax.experimental.pallas import tpu as pltpu
from jax.sharding import PartitionSpec as P

R = 68
HALF = R // 2
F = 1 + R + R * (R + 1) // 2
OWN = (F + 1) // 8
PAD = -(-OWN // 16) * 16
GROUPS = 4
NX, NZ, NT = 4, 8, 8
CHUNKS = (1024, 2048) + (3072,) * 9 + (1024, 512, 512)
SLOTS = (0, 1, 3, 2)
LAST = 2432
MESH = pl.DeviceIdType.MESH
CONTRACT_LANES = (((1,), (1,)), ((), ()))


def quadratic_rows():
    starts, at = [], 1 + R
    for i in range(R):
        starts.append(at)
        at += R - i
    return starts


def split(value):
    high = value.astype(jnp.bfloat16)
    return high, (value - high.astype(jnp.float32)).astype(jnp.bfloat16)


def dot(a, b):
    return lax.dot_general(a, b, CONTRACT_LANES, preferred_element_type=jnp.float32)


def tiles():
    return [(at, min(at + 256, LAST)) for at in range(0, LAST, 256)]


def pair_products(own, hi, lo):
    both = dot(own, hi)
    return both[:PAD] + both[PAD:] + dot(own[:PAD], lo)


def single_products(own, hi, lo):
    high = own[:PAD]
    whole = dot(jnp.concatenate([high, high], axis=1), jnp.concatenate([hi, lo], axis=1))
    return whole + dot(own[PAD:], hi)


def project_and_share(
    snap_hbm, pod_hbm, pen_hbm, part_ref, own_ref, late_ref, modes,
    snap, pod, pen, xbuf, zbuf, tbuf, feat, load_sem, pen_sem, send_sem, recv_sem
):
    loads, at = [], 0
    for i, width in enumerate(CHUNKS):
        cols = slice(at, at + width)
        at += width
        loads.append((
            cols,
            pltpu.make_async_copy(snap_hbm.at[:, cols], snap.at[:, cols], load_sem.at[0, i]),
            pltpu.make_async_copy(pod_hbm.at[:, cols], pod.at[:, cols], load_sem.at[1, i]),
        ))
    for _, first, second in loads[:5]:
        first.start()
        second.start()

    space, tm = lax.axis_index("space"), lax.axis_index("tm")
    z, x = space // NX, lax.rem(space, NX)
    y, core = tm // 2, lax.rem(tm, 2)
    x_peers = [(z * NX + k + (x <= k).astype(jnp.int32), tm) for k in range(NX - 1)]
    z_peers = [((k + (z <= k).astype(jnp.int32)) * NX + x, tm) for k in range(NZ - 1)]
    chips = [lax.rem(y + k, GROUPS) for k in range(GROUPS)]
    sibling = (space, 2 * y + (1 - core))
    y_peers = [k + (y <= k).astype(jnp.int32) for k in range(GROUPS - 1)]
    t_peers = [sibling] + [(space, 2 * chip + c) for chip in y_peers for c in range(2)]

    barrier = pltpu.get_barrier_semaphore()
    peers = z_peers + t_peers + x_peers
    for peer in peers:
        pl.semaphore_signal(barrier, inc=1, device_id=peer, device_id_type=MESH)

    for _, first, second in loads[5:]:
        first.start()
        second.start()
    pen_copy = pltpu.make_async_copy(pen_hbm, pen, pen_sem)
    pen_copy.start()

    for g in range(GROUPS):
        place(feat, late_ref, g, slice(0, 1), jnp.ones((1, 128), jnp.float32))
    modes[:, R:80] = jnp.zeros((GROUPS, 80 - R, 128), jnp.float32)

    total = jnp.zeros((R, snap_hbm.shape[0]), jnp.float32)
    for cols, first, second in loads:
        first.wait()
        second.wait()
        total = total + dot(pod[:, cols], snap[:, cols])
    packed = jnp.concatenate([total[:HALF], total[HALF:]], axis=1)

    pl.semaphore_wait(barrier, len(peers))

    def send(buf, rank, peer, way, phase):
        pltpu.make_async_remote_copy(
            src_ref=buf.at[rank],
            dst_ref=buf.at[rank],
            send_sem=send_sem.at[way],
            recv_sem=recv_sem.at[phase],
            device_id=peer,
            device_id_type=MESH,
        ).start()

    def arrived(buf, at, count, sem):
        slots = buf.at[pl.ds(at, count)]
        pltpu.make_async_copy(slots, slots, sem).wait()

    xbuf[x] = packed
    for peer in x_peers:
        send(xbuf, x, peer, 0, 0)
    arrived(xbuf, 0, NX - 1, recv_sem.at[0])
    zbuf[z] = (xbuf[0] + xbuf[1]) + (xbuf[2] + xbuf[3])
    for peer in z_peers:
        send(zbuf, z, peer, 1, 1)
    arrived(zbuf, 0, NZ - 1, recv_sem.at[1])
    tbuf[tm] = ((zbuf[0] + zbuf[1]) + (zbuf[2] + zbuf[3])) + (
        (zbuf[4] + zbuf[5]) + (zbuf[6] + zbuf[7])
    )
    send(tbuf, tm, sibling, 2, 2)
    for chip in y_peers:
        for c in range(2):
            send(tbuf, tm, (space, 2 * chip + c), 2, 2 + lax.rem(y - chip + GROUPS, GROUPS))

    half_lane = lax.broadcasted_iota(jnp.int32, (HALF, 128), 1) < 64
    first_row = tm * OWN

    def build(g):
        chip = chips[SLOTS[g]]
        a, b = tbuf[2 * chip], tbuf[2 * chip + 1]
        modes[g, 0:HALF] = jnp.where(half_lane, a, pltpu.roll(b, 64, 1))
        modes[g, HALF:R] = jnp.where(half_lane, pltpu.roll(a, 64, 1), b)
        place(feat, late_ref, g, slice(1, 1 + R), modes[g, :R])
        for i, at in enumerate(quadratic_rows()):
            rows = -(-(R - i) // 8) * 8
            place(feat, late_ref, g, slice(at, at + rows), modes[g, i : i + rows] * modes[g, i : i + 1])
        place(feat, late_ref, g, slice(F, LAST), jnp.zeros((LAST - F, 128), jnp.float32))
        mine = pl.ds(first_row, PAD)
        value = (feat[g, mine] if g < 2 else late_ref[g - 2, mine]) * (1.0 / (GROUPS * 128))
        lanes = slice(g * 128, (g + 1) * 128)
        own_ref[0:PAD, lanes], own_ref[PAD : 2 * PAD, lanes] = split(value)

    arrived(tbuf, sibling[1], 1, recv_sem.at[2])
    build(0)
    pen_copy.wait()
    own = own_ref[:, 0:128]
    for at, end in tiles():
        penalty = pen[at : min(end, F)][None, :]
        if end > F:
            penalty = jnp.concatenate([penalty, jnp.zeros((1, end - F), jnp.float32)], axis=1)
        row = lax.broadcasted_iota(jnp.int32, (PAD, end - at), 0) + first_row
        col = lax.broadcasted_iota(jnp.int32, (PAD, end - at), 1) + at
        diagonal = jnp.where(row == col, penalty, 0.0)
        part_ref[:, at:end] = single_products(own, *split(feat[0, at:end])) + diagonal
    arrived(tbuf, 2 * chips[1], 2, recv_sem.at[3])
    build(1)
    own = own_ref[:, 128:256]
    for at, end in tiles():
        part_ref[:, at:end] += single_products(own, *split(feat[1, at:end]))
    arrived(tbuf, 2 * chips[3], 2, recv_sem.at[5])
    build(2)
    arrived(tbuf, 2 * chips[2], 2, recv_sem.at[4])
    build(3)

    for way, buf, count in ((0, xbuf, NX - 1), (1, zbuf, NZ - 1), (2, tbuf, NT - 1)):
        arrived(buf, 0, count, send_sem.at[way])


def place(feat, late_ref, g, rows, value):
    if g < 2:
        feat[g, rows] = value
    else:
        late_ref[g - 2, rows] = value


def normal_equations(
    part_ref, own_ref, late_ref, modes, normal_ref, rhs_ref, state_ref, rate_ref, turned, obuf, rbuf, mine, sem
):
    space, tm = lax.axis_index("space"), lax.axis_index("tm")
    snaps = GROUPS * 128
    own = own_ref[:, snaps // 2 :]
    copies = []

    def write(source, target, n):
        copies.append(pltpu.make_async_copy(source, target, sem.at[n]))
        copies[-1].start()

    for n, (at, end) in enumerate(tiles()):
        cols = slice(at, min(end, F))
        value = jnp.concatenate([late_ref[0, at:end], late_ref[1, at:end]], axis=1)
        gram = pair_products(own, *split(value)) + part_ref[:, at:end]
        obuf[:, cols] = gram[:OWN, : cols.stop - at]
        write(obuf.at[:, cols], normal_ref.at[:, cols], n)

        if n == 6:
            order = [modes[SLOTS.index(k), :72] for k in range(GROUPS)]
            whole = jnp.concatenate(order, axis=1)
            when = lax.rem(lax.broadcasted_iota(jnp.int32, (72, snaps), 1) + (tm // 2) * 128, snaps)
            first, last = when == 0, when == snaps - 1
            after = jnp.where(last, whole, pltpu.roll(whole, snaps - 1, 1))
            before = jnp.where(first, whole, pltpu.roll(whole, 1, 1))
            rate = (after - before) * jnp.where(first | last, 1.0, 0.5)
            rate = jnp.concatenate([rate, jnp.zeros((56, snaps), jnp.float32)], axis=0)
            turned[0] = jnp.concatenate([whole[:, :128], jnp.zeros((56, 128), jnp.float32)], axis=0).T
            turned[1] = rate[:, :128].T
            here = lax.rem(tm, 2) * 64 + 2 * space
            mine[0, 0] = turned[0, pl.ds(here, 2)][:, :R]
            mine[1, 0] = turned[1, pl.ds(here, 2)][:, :R]
            write(mine.at[0], state_ref, len(tiles()) + 1)
            write(mine.at[1], rate_ref, len(tiles()) + 2)
            rate = jnp.concatenate([rate[:, 128 * k : 128 * (k + 1)] for k in SLOTS], axis=1)
            rhs = pair_products(own_ref[...], *split(rate))
            rbuf[...] = rhs[:OWN].T[:R]
            write(rbuf, rhs_ref, len(tiles()))
    for copy in copies:
        copy.wait()


def shards(snapshots, pod_basis, penalty):
    group, dofs = snapshots.shape
    snaps = GROUPS * 128
    hbm = pl.BlockSpec(memory_space=pltpu.HBM)
    vmem = pl.BlockSpec(memory_space=pltpu.VMEM)
    shared = pl.pallas_call(
        project_and_share,
        out_shape=[
            pltpu.VMEM((PAD, LAST), jnp.float32),
            pltpu.VMEM((2 * PAD, snaps), jnp.bfloat16),
            pltpu.VMEM((2, LAST, 128), jnp.float32),
            pltpu.VMEM((GROUPS, 80, 128), jnp.float32),
        ],
        in_specs=[hbm, hbm, hbm],
        out_specs=[vmem] * 4,
        scratch_shapes=[
            pltpu.VMEM((group, dofs), jnp.bfloat16),
            pltpu.VMEM((R, dofs), jnp.bfloat16),
            pltpu.VMEM((F,), jnp.float32),
            pltpu.VMEM((NX, HALF, 128), jnp.float32),
            pltpu.VMEM((NZ, HALF, 128), jnp.float32),
            pltpu.VMEM((NT, HALF, 128), jnp.float32),
            pltpu.VMEM((2, LAST, 128), jnp.float32),
            pltpu.SemaphoreType.DMA((2, len(CHUNKS))),
            pltpu.SemaphoreType.DMA,
            pltpu.SemaphoreType.DMA((3,)),
            pltpu.SemaphoreType.DMA((6,)),
        ],
        compiler_params=pltpu.CompilerParams(
            collective_id=0, has_side_effects=True, vmem_limit_bytes=53 << 20
        ),
        name="project_and_share",
    )(snapshots, pod_basis, penalty)
    normal, rhs, state, rates = pl.pallas_call(
        normal_equations,
        out_shape=[
            jax.ShapeDtypeStruct((OWN, F), jnp.float32),
            jax.ShapeDtypeStruct((R, OWN), jnp.float32),
            jax.ShapeDtypeStruct((1, 2, R), jnp.float32),
            jax.ShapeDtypeStruct((1, 2, R), jnp.float32),
        ],
        in_specs=[vmem] * 4,
        out_specs=[hbm] * 4,
        scratch_shapes=[
            pltpu.VMEM((2, 128, 128), jnp.float32),
            pltpu.VMEM((OWN, F), jnp.float32),
            pltpu.VMEM((R, OWN), jnp.float32),
            pltpu.VMEM((2, 1, 2, R), jnp.float32),
            pltpu.SemaphoreType.DMA((len(tiles()) + 3,)),
        ],
        compiler_params=pltpu.CompilerParams(vmem_limit_bytes=16 << 20),
        name="normal_equations",
    )(*shared)
    return normal, rhs.T, state, rates


def solution(mesh):
    return jax.shard_map(
        shards,
        mesh=mesh,
        in_specs=(P("tm", "space"), P(None, "space"), P()),
        out_specs=(P("tm", None), P("tm", None), P("tm", "space", None), P("tm", "space", None)),
        check_vma=False,
    )
```

```python
import functools

import jax
import jax.numpy as jnp
from jax import lax
from jax.experimental import pallas as pl
from jax.experimental.pallas import tpu as pltpu
from jax.sharding import PartitionSpec as P

R = 68
HALF = R // 2
F = 1 + R + R * (R + 1) // 2
OWN = (F + 1) // 8
PAD = -(-OWN // 16) * 16
GROUPS = 4
NX, NZ, NT = 4, 8, 8
CHUNKS = (1024, 2048) + (3072,) * 9 + (1024, 512, 512)
SLOTS = (0, 1, 3, 2)
LAST = 2432
MESH = pl.DeviceIdType.MESH
CONTRACT_LANES = (((1,), (1,)), ((), ()))


def quadratic_rows():
    starts, at = [], 1 + R
    for i in range(R):
        starts.append(at)
        at += R - i
    return starts


def split(value):
    high = value.astype(jnp.bfloat16)
    return high, (value - high.astype(jnp.float32)).astype(jnp.bfloat16)


def dot(a, b):
    return lax.dot_general(a, b, CONTRACT_LANES, preferred_element_type=jnp.float32)


def tiles():
    return [(at, min(at + 256, LAST)) for at in range(0, LAST, 256)]


def pair_products(own, hi, lo):
    both = dot(own, hi)
    return both[:PAD] + both[PAD:] + dot(own[:PAD], lo)


def single_products(own, hi, lo):
    high = own[:PAD]
    whole = dot(jnp.concatenate([high, high], axis=1), jnp.concatenate([hi, lo], axis=1))
    return whole + dot(own[PAD:], hi)


def project_and_share(
    snap_hbm, pod_hbm, pen_hbm, part_ref, own_ref, late_ref, modes,
    snap, pod, pen, xbuf, zbuf, tbuf, feat, load_sem, pen_sem, send_sem, recv_sem
):
    loads, at = [], 0
    for i, width in enumerate(CHUNKS):
        cols = slice(at, at + width)
        at += width
        loads.append((
            cols,
            pltpu.make_async_copy(snap_hbm.at[:, cols], snap.at[:, cols], load_sem.at[0, i]),
            pltpu.make_async_copy(pod_hbm.at[:, cols], pod.at[:, cols], load_sem.at[1, i]),
        ))
    for _, first, second in loads[:5]:
        first.start()
        second.start()

    space, tm = lax.axis_index("space"), lax.axis_index("tm")
    z, x = space // NX, lax.rem(space, NX)
    y, core = tm // 2, lax.rem(tm, 2)
    x_peers = [(z * NX + k + (x <= k).astype(jnp.int32), tm) for k in range(NX - 1)]
    z_peers = [((k + (z <= k).astype(jnp.int32)) * NX + x, tm) for k in range(NZ - 1)]
    chips = [lax.rem(y + k, GROUPS) for k in range(GROUPS)]
    sibling = (space, 2 * y + (1 - core))
    y_peers = [k + (y <= k).astype(jnp.int32) for k in range(GROUPS - 1)]
    t_peers = [sibling] + [(space, 2 * chip + c) for chip in y_peers for c in range(2)]

    barrier = pltpu.get_barrier_semaphore()
    peers = z_peers + t_peers + x_peers
    for peer in peers:
        pl.semaphore_signal(barrier, inc=1, device_id=peer, device_id_type=MESH)

    for _, first, second in loads[5:]:
        first.start()
        second.start()
    pen_copy = pltpu.make_async_copy(pen_hbm, pen, pen_sem)
    pen_copy.start()

    for g in range(GROUPS):
        place(feat, late_ref, g, slice(0, 1), jnp.ones((1, 128), jnp.float32))
    modes[:, R:80] = jnp.zeros((GROUPS, 80 - R, 128), jnp.float32)

    total = jnp.zeros((R, snap_hbm.shape[0]), jnp.float32)
    for cols, first, second in loads:
        first.wait()
        second.wait()
        total = total + dot(pod[:, cols], snap[:, cols])
    packed = jnp.concatenate([total[:HALF], total[HALF:]], axis=1)

    pl.semaphore_wait(barrier, len(peers))

    def send(buf, rank, peer, way, phase):
        pltpu.make_async_remote_copy(
            src_ref=buf.at[rank],
            dst_ref=buf.at[rank],
            send_sem=send_sem.at[way],
            recv_sem=recv_sem.at[phase],
            device_id=peer,
            device_id_type=MESH,
        ).start()

    def arrived(buf, at, count, sem):
        slots = buf.at[pl.ds(at, count)]
        pltpu.make_async_copy(slots, slots, sem).wait()

    xbuf[x] = packed
    for peer in x_peers:
        send(xbuf, x, peer, 0, 0)
    arrived(xbuf, 0, NX - 1, recv_sem.at[0])
    zbuf[z] = (xbuf[0] + xbuf[1]) + (xbuf[2] + xbuf[3])
    for peer in z_peers:
        send(zbuf, z, peer, 1, 1)
    arrived(zbuf, 0, NZ - 1, recv_sem.at[1])
    tbuf[tm] = ((zbuf[0] + zbuf[1]) + (zbuf[2] + zbuf[3])) + (
        (zbuf[4] + zbuf[5]) + (zbuf[6] + zbuf[7])
    )
    send(tbuf, tm, sibling, 2, 2)
    for chip in y_peers:
        for c in range(2):
            send(tbuf, tm, (space, 2 * chip + c), 2, 2 + lax.rem(y - chip + GROUPS, GROUPS))

    half_lane = lax.broadcasted_iota(jnp.int32, (HALF, 128), 1) < 64
    first_row = tm * OWN

    def build(g):
        chip = chips[SLOTS[g]]
        a, b = tbuf[2 * chip], tbuf[2 * chip + 1]
        modes[g, 0:HALF] = jnp.where(half_lane, a, pltpu.roll(b, 64, 1))
        modes[g, HALF:R] = jnp.where(half_lane, pltpu.roll(a, 64, 1), b)
        place(feat, late_ref, g, slice(1, 1 + R), modes[g, :R])
        for i, at in enumerate(quadratic_rows()):
            rows = -(-(R - i) // 8) * 8
            place(feat, late_ref, g, slice(at, at + rows), modes[g, i : i + rows] * modes[g, i : i + 1])
        place(feat, late_ref, g, slice(F, LAST), jnp.zeros((LAST - F, 128), jnp.float32))
        mine = pl.ds(first_row, PAD)
        value = (feat[g, mine] if g < 2 else late_ref[g - 2, mine]) * (1.0 / (GROUPS * 128))
        lanes = slice(g * 128, (g + 1) * 128)
        own_ref[0:PAD, lanes], own_ref[PAD : 2 * PAD, lanes] = split(value)

    arrived(tbuf, sibling[1], 1, recv_sem.at[2])
    build(0)
    pen_copy.wait()
    own = own_ref[:, 0:128]
    for at, end in tiles():
        penalty = pen[at : min(end, F)][None, :]
        if end > F:
            penalty = jnp.concatenate([penalty, jnp.zeros((1, end - F), jnp.float32)], axis=1)
        row = lax.broadcasted_iota(jnp.int32, (PAD, end - at), 0) + first_row
        col = lax.broadcasted_iota(jnp.int32, (PAD, end - at), 1) + at
        diagonal = jnp.where(row == col, penalty, 0.0)
        part_ref[:, at:end] = single_products(own, *split(feat[0, at:end])) + diagonal
    arrived(tbuf, 2 * chips[1], 2, recv_sem.at[3])
    build(1)
    own = own_ref[:, 128:256]
    for at, end in tiles():
        part_ref[:, at:end] += single_products(own, *split(feat[1, at:end]))
    arrived(tbuf, 2 * chips[3], 2, recv_sem.at[5])
    build(2)
    arrived(tbuf, 2 * chips[2], 2, recv_sem.at[4])
    build(3)

    for way, buf, count in ((0, xbuf, NX - 1), (1, zbuf, NZ - 1), (2, tbuf, NT - 1)):
        arrived(buf, 0, count, send_sem.at[way])


def place(feat, late_ref, g, rows, value):
    if g < 2:
        feat[g, rows] = value
    else:
        late_ref[g - 2, rows] = value


def normal_equations(
    part_ref, own_ref, late_ref, modes, normal_ref, rhs_ref, state_ref, rate_ref, turned, obuf, rbuf, mine, sem
):
    space, tm = lax.axis_index("space"), lax.axis_index("tm")
    snaps = GROUPS * 128
    own = own_ref[:, snaps // 2 :]
    copies = []

    def write(source, target, n):
        copies.append(pltpu.make_async_copy(source, target, sem.at[n]))
        copies[-1].start()

    for n, (at, end) in enumerate(tiles()):
        cols = slice(at, min(end, F))
        value = jnp.concatenate([late_ref[0, at:end], late_ref[1, at:end]], axis=1)
        high, low = split(value)
        if end == LAST:
            high = jnp.concatenate([high, rate_hi[:, snaps // 2 :]], axis=0)
            low = jnp.concatenate([low, rate_lo[:, snaps // 2 :]], axis=0)
            gram = pair_products(own, high, low)
            rhs = gram[:, end - at :] + rhs_early
            gram = gram[:, : end - at] + part_ref[:, at:end]
            rbuf[...] = rhs[:OWN].T[:R]
            write(rbuf, rhs_ref, len(tiles()))
        else:
            gram = pair_products(own, high, low) + part_ref[:, at:end]
        obuf[:, cols] = gram[:OWN, : cols.stop - at]
        write(obuf.at[:, cols], normal_ref.at[:, cols], n)

        if n == 8:
            order = [modes[SLOTS.index(k), :72] for k in range(GROUPS)]
            whole = jnp.concatenate(order, axis=1)
            when = lax.rem(lax.broadcasted_iota(jnp.int32, (72, snaps), 1) + (tm // 2) * 128, snaps)
            first, last = when == 0, when == snaps - 1
            after = jnp.where(last, whole, pltpu.roll(whole, snaps - 1, 1))
            before = jnp.where(first, whole, pltpu.roll(whole, 1, 1))
            rate = (after - before) * jnp.where(first | last, 1.0, 0.5)
            rate = jnp.concatenate([rate, jnp.zeros((56, snaps), jnp.float32)], axis=0)
            turned[0] = jnp.concatenate([whole[:, :128], jnp.zeros((56, 128), jnp.float32)], axis=0).T
            turned[1] = rate[:, :128].T
            here = lax.rem(tm, 2) * 64 + 2 * space
            mine[0, 0] = turned[0, pl.ds(here, 2)][:, :R]
            mine[1, 0] = turned[1, pl.ds(here, 2)][:, :R]
            write(mine.at[0], state_ref, len(tiles()) + 1)
            write(mine.at[1], rate_ref, len(tiles()) + 2)
            rate = jnp.concatenate([rate[:, 128 * k : 128 * (k + 1)] for k in SLOTS], axis=1)
            rate_hi, rate_lo = split(rate)
            rhs_early = pair_products(own_ref[:, : snaps // 2], rate_hi[:, : snaps // 2], rate_lo[:, : snaps // 2])
    for copy in copies:
        copy.wait()


def shards(snapshots, pod_basis, penalty):
    group, dofs = snapshots.shape
    snaps = GROUPS * 128
    hbm = pl.BlockSpec(memory_space=pltpu.HBM)
    vmem = pl.BlockSpec(memory_space=pltpu.VMEM)
    shared = pl.pallas_call(
        project_and_share,
        out_shape=[
            pltpu.VMEM((PAD, LAST), jnp.float32),
            pltpu.VMEM((2 * PAD, snaps), jnp.bfloat16),
            pltpu.VMEM((2, LAST, 128), jnp.float32),
            pltpu.VMEM((GROUPS, 80, 128), jnp.float32),
        ],
        in_specs=[hbm, hbm, hbm],
        out_specs=[vmem] * 4,
        scratch_shapes=[
            pltpu.VMEM((group, dofs), jnp.bfloat16),
            pltpu.VMEM((R, dofs), jnp.bfloat16),
            pltpu.VMEM((F,), jnp.float32),
            pltpu.VMEM((NX, HALF, 128), jnp.float32),
            pltpu.VMEM((NZ, HALF, 128), jnp.float32),
            pltpu.VMEM((NT, HALF, 128), jnp.float32),
            pltpu.VMEM((2, LAST, 128), jnp.float32),
            pltpu.SemaphoreType.DMA((2, len(CHUNKS))),
            pltpu.SemaphoreType.DMA,
            pltpu.SemaphoreType.DMA((3,)),
            pltpu.SemaphoreType.DMA((6,)),
        ],
        compiler_params=pltpu.CompilerParams(
            collective_id=0, has_side_effects=True, vmem_limit_bytes=53 << 20
        ),
        name="project_and_share",
    )(snapshots, pod_basis, penalty)
    normal, rhs, state, rates = pl.pallas_call(
        normal_equations,
        out_shape=[
            jax.ShapeDtypeStruct((OWN, F), jnp.float32),
            jax.ShapeDtypeStruct((R, OWN), jnp.float32),
            jax.ShapeDtypeStruct((1, 2, R), jnp.float32),
            jax.ShapeDtypeStruct((1, 2, R), jnp.float32),
        ],
        in_specs=[vmem] * 4,
        out_specs=[hbm] * 4,
        scratch_shapes=[
            pltpu.VMEM((2, 128, 128), jnp.float32),
            pltpu.VMEM((OWN, F), jnp.float32),
            pltpu.VMEM((R, OWN), jnp.float32),
            pltpu.VMEM((2, 1, 2, R), jnp.float32),
            pltpu.SemaphoreType.DMA((len(tiles()) + 3,)),
        ],
        compiler_params=pltpu.CompilerParams(vmem_limit_bytes=16 << 20),
        name="normal_equations",
    )(*shared)
    return normal, rhs.T, state, rates


def solution(mesh):
    return jax.shard_map(
        shards,
        mesh=mesh,
        in_specs=(P("tm", "space"), P(None, "space"), P()),
        out_specs=(P("tm", None), P("tm", None), P("tm", "space", None), P("tm", "space", None)),
        check_vma=False,
    )
```

```python
import functools

import jax
import jax.numpy as jnp
from jax import lax
from jax.experimental import pallas as pl
from jax.experimental.pallas import tpu as pltpu
from jax.sharding import PartitionSpec as P

R = 68
HALF = R // 2
F = 1 + R + R * (R + 1) // 2
OWN = (F + 1) // 8
PAD = -(-OWN // 16) * 16
GROUPS = 4
NX, NZ, NT = 4, 8, 8
CHUNKS = (1024, 3072) + (4096,) * 6 + (2048, 1024, 1024)
SLOTS = (0, 1, 3, 2)
LAST = 2432
MESH = pl.DeviceIdType.MESH
CONTRACT_LANES = (((1,), (1,)), ((), ()))


def quadratic_rows():
    starts, at = [], 1 + R
    for i in range(R):
        starts.append(at)
        at += R - i
    return starts


def split(value):
    high = value.astype(jnp.bfloat16)
    return high, (value - high.astype(jnp.float32)).astype(jnp.bfloat16)


def dot(a, b):
    return lax.dot_general(a, b, CONTRACT_LANES, preferred_element_type=jnp.float32)


def tiles():
    return [(at, min(at + 256, LAST)) for at in range(0, LAST, 256)]


def pair_products(own, hi, lo):
    both = dot(own, hi)
    return both[:PAD] + both[PAD:] + dot(own[:PAD], lo)


def single_products(own, hi, lo):
    high = own[:PAD]
    whole = dot(jnp.concatenate([high, high], axis=1), jnp.concatenate([hi, lo], axis=1))
    return whole + dot(own[PAD:], hi)


def project_and_share(
    snap_hbm, pod_hbm, pen_hbm, part_ref, own_ref, late_ref, modes,
    snap, pod, pen, xbuf, zbuf, tbuf, feat, load_sem, pen_sem, send_sem, recv_sem
):
    loads, at = [], 0
    for i, width in enumerate(CHUNKS):
        cols = slice(at, at + width)
        at += width
        loads.append((
            cols,
            pltpu.make_async_copy(snap_hbm.at[:, cols], snap.at[:, cols], load_sem.at[0, i]),
            pltpu.make_async_copy(pod_hbm.at[:, cols], pod.at[:, cols], load_sem.at[1, i]),
        ))
    for _, first, second in loads[:5]:
        first.start()
        second.start()

    space, tm = lax.axis_index("space"), lax.axis_index("tm")
    z, x = space // NX, lax.rem(space, NX)
    y, core = tm // 2, lax.rem(tm, 2)
    x_peers = [(z * NX + k + (x <= k).astype(jnp.int32), tm) for k in range(NX - 1)]
    z_peers = [((k + (z <= k).astype(jnp.int32)) * NX + x, tm) for k in range(NZ - 1)]
    chips = [lax.rem(y + k, GROUPS) for k in range(GROUPS)]
    sibling = (space, 2 * y + (1 - core))
    y_peers = [k + (y <= k).astype(jnp.int32) for k in range(GROUPS - 1)]
    t_peers = [sibling] + [(space, 2 * chip + c) for chip in y_peers for c in range(2)]

    barrier = pltpu.get_barrier_semaphore()
    peers = z_peers + t_peers + x_peers
    for peer in peers:
        pl.semaphore_signal(barrier, inc=1, device_id=peer, device_id_type=MESH)

    for _, first, second in loads[5:]:
        first.start()
        second.start()
    pen_copy = pltpu.make_async_copy(pen_hbm, pen, pen_sem)
    pen_copy.start()

    for g in range(GROUPS):
        place(feat, late_ref, g, slice(0, 1), jnp.ones((1, 128), jnp.float32))
    modes[:, R:80] = jnp.zeros((GROUPS, 80 - R, 128), jnp.float32)

    total = jnp.zeros((R, snap_hbm.shape[0]), jnp.float32)
    for cols, first, second in loads:
        first.wait()
        second.wait()
        total = total + dot(pod[:, cols], snap[:, cols])
    packed = jnp.concatenate([total[:HALF], total[HALF:]], axis=1)

    pl.semaphore_wait(barrier, len(peers))

    def send(buf, rank, peer, way, phase):
        pltpu.make_async_remote_copy(
            src_ref=buf.at[rank],
            dst_ref=buf.at[rank],
            send_sem=send_sem.at[way],
            recv_sem=recv_sem.at[phase],
            device_id=peer,
            device_id_type=MESH,
        ).start()

    def arrived(buf, at, count, sem):
        slots = buf.at[pl.ds(at, count)]
        pltpu.make_async_copy(slots, slots, sem).wait()

    xbuf[x] = packed
    for peer in x_peers:
        send(xbuf, x, peer, 0, 0)
    arrived(xbuf, 0, NX - 1, recv_sem.at[0])
    zbuf[z] = (xbuf[0] + xbuf[1]) + (xbuf[2] + xbuf[3])
    for peer in z_peers:
        send(zbuf, z, peer, 1, 1)
    arrived(zbuf, 0, NZ - 1, recv_sem.at[1])
    tbuf[tm] = ((zbuf[0] + zbuf[1]) + (zbuf[2] + zbuf[3])) + (
        (zbuf[4] + zbuf[5]) + (zbuf[6] + zbuf[7])
    )
    send(tbuf, tm, sibling, 2, 2)
    for chip in y_peers:
        for c in range(2):
            send(tbuf, tm, (space, 2 * chip + c), 2, 2 + lax.rem(y - chip + GROUPS, GROUPS))

    half_lane = lax.broadcasted_iota(jnp.int32, (HALF, 128), 1) < 64
    first_row = tm * OWN

    def build(g):
        chip = chips[SLOTS[g]]
        a, b = tbuf[2 * chip], tbuf[2 * chip + 1]
        modes[g, 0:HALF] = jnp.where(half_lane, a, pltpu.roll(b, 64, 1))
        modes[g, HALF:R] = jnp.where(half_lane, pltpu.roll(a, 64, 1), b)
        place(feat, late_ref, g, slice(1, 1 + R), modes[g, :R])
        for i, at in enumerate(quadratic_rows()):
            rows = -(-(R - i) // 8) * 8
            place(feat, late_ref, g, slice(at, at + rows), modes[g, i : i + rows] * modes[g, i : i + 1])
        place(feat, late_ref, g, slice(F, LAST), jnp.zeros((LAST - F, 128), jnp.float32))
        mine = pl.ds(first_row, PAD)
        value = (feat[g, mine] if g < 2 else late_ref[g - 2, mine]) * (1.0 / (GROUPS * 128))
        lanes = slice(g * 128, (g + 1) * 128)
        own_ref[0:PAD, lanes], own_ref[PAD : 2 * PAD, lanes] = split(value)

    arrived(tbuf, sibling[1], 1, recv_sem.at[2])
    build(0)
    pen_copy.wait()
    own = own_ref[:, 0:128]
    for at, end in tiles():
        penalty = pen[at : min(end, F)][None, :]
        if end > F:
            penalty = jnp.concatenate([penalty, jnp.zeros((1, end - F), jnp.float32)], axis=1)
        row = lax.broadcasted_iota(jnp.int32, (PAD, end - at), 0) + first_row
        col = lax.broadcasted_iota(jnp.int32, (PAD, end - at), 1) + at
        diagonal = jnp.where(row == col, penalty, 0.0)
        part_ref[:, at:end] = single_products(own, *split(feat[0, at:end])) + diagonal
    arrived(tbuf, 2 * chips[1], 2, recv_sem.at[3])
    build(1)
    own = own_ref[:, 128:256]
    for at, end in tiles():
        part_ref[:, at:end] += single_products(own, *split(feat[1, at:end]))
    arrived(tbuf, 2 * chips[3], 2, recv_sem.at[5])
    build(2)
    arrived(tbuf, 2 * chips[2], 2, recv_sem.at[4])
    build(3)

    for way, buf, count in ((0, xbuf, NX - 1), (1, zbuf, NZ - 1), (2, tbuf, NT - 1)):
        arrived(buf, 0, count, send_sem.at[way])


def place(feat, late_ref, g, rows, value):
    if g < 2:
        feat[g, rows] = value
    else:
        late_ref[g - 2, rows] = value


def normal_equations(
    part_ref, own_ref, late_ref, modes, normal_ref, rhs_ref, state_ref, rate_ref, turned, obuf, rbuf, mine, sem
):
    space, tm = lax.axis_index("space"), lax.axis_index("tm")
    snaps = GROUPS * 128
    own = own_ref[:, snaps // 2 :]
    copies = []

    def write(source, target, n):
        copies.append(pltpu.make_async_copy(source, target, sem.at[n]))
        copies[-1].start()

    for n, (at, end) in enumerate(tiles()):
        cols = slice(at, min(end, F))
        value = jnp.concatenate([late_ref[0, at:end], late_ref[1, at:end]], axis=1)
        high, low = split(value)
        if end == LAST:
            high = jnp.concatenate([high, rate_hi[:, snaps // 2 :]], axis=0)
            low = jnp.concatenate([low, rate_lo[:, snaps // 2 :]], axis=0)
            gram = pair_products(own, high, low)
            rhs = gram[:, end - at :] + rhs_early
            gram = gram[:, : end - at] + part_ref[:, at:end]
            rbuf[...] = rhs[:OWN].T[:R]
            write(rbuf, rhs_ref, len(tiles()))
        else:
            gram = pair_products(own, high, low) + part_ref[:, at:end]
        obuf[:, cols] = gram[:OWN, : cols.stop - at]
        write(obuf.at[:, cols], normal_ref.at[:, cols], n)

        if n == 8:
            order = [modes[SLOTS.index(k), :72] for k in range(GROUPS)]
            whole = jnp.concatenate(order, axis=1)
            when = lax.rem(lax.broadcasted_iota(jnp.int32, (72, snaps), 1) + (tm // 2) * 128, snaps)
            first, last = when == 0, when == snaps - 1
            after = jnp.where(last, whole, pltpu.roll(whole, snaps - 1, 1))
            before = jnp.where(first, whole, pltpu.roll(whole, 1, 1))
            rate = (after - before) * jnp.where(first | last, 1.0, 0.5)
            rate = jnp.concatenate([rate, jnp.zeros((56, snaps), jnp.float32)], axis=0)
            turned[0] = jnp.concatenate([whole[:, :128], jnp.zeros((56, 128), jnp.float32)], axis=0).T
            turned[1] = rate[:, :128].T
            here = lax.rem(tm, 2) * 64 + 2 * space
            mine[0, 0] = turned[0, pl.ds(here, 2)][:, :R]
            mine[1, 0] = turned[1, pl.ds(here, 2)][:, :R]
            write(mine.at[0], state_ref, len(tiles()) + 1)
            write(mine.at[1], rate_ref, len(tiles()) + 2)
            rate = jnp.concatenate([rate[:, 128 * k : 128 * (k + 1)] for k in SLOTS], axis=1)
            rate_hi, rate_lo = split(rate)
            rhs_early = pair_products(own_ref[:, : snaps // 2], rate_hi[:, : snaps // 2], rate_lo[:, : snaps // 2])
    for copy in copies:
        copy.wait()


def shards(snapshots, pod_basis, penalty):
    group, dofs = snapshots.shape
    snaps = GROUPS * 128
    hbm = pl.BlockSpec(memory_space=pltpu.HBM)
    vmem = pl.BlockSpec(memory_space=pltpu.VMEM)
    shared = pl.pallas_call(
        project_and_share,
        out_shape=[
            pltpu.VMEM((PAD, LAST), jnp.float32),
            pltpu.VMEM((2 * PAD, snaps), jnp.bfloat16),
            pltpu.VMEM((2, LAST, 128), jnp.float32),
            pltpu.VMEM((GROUPS, 80, 128), jnp.float32),
        ],
        in_specs=[hbm, hbm, hbm],
        out_specs=[vmem] * 4,
        scratch_shapes=[
            pltpu.VMEM((group, dofs), jnp.bfloat16),
            pltpu.VMEM((R, dofs), jnp.bfloat16),
            pltpu.VMEM((F,), jnp.float32),
            pltpu.VMEM((NX, HALF, 128), jnp.float32),
            pltpu.VMEM((NZ, HALF, 128), jnp.float32),
            pltpu.VMEM((NT, HALF, 128), jnp.float32),
            pltpu.VMEM((2, LAST, 128), jnp.float32),
            pltpu.SemaphoreType.DMA((2, len(CHUNKS))),
            pltpu.SemaphoreType.DMA,
            pltpu.SemaphoreType.DMA((3,)),
            pltpu.SemaphoreType.DMA((6,)),
        ],
        compiler_params=pltpu.CompilerParams(
            collective_id=0, has_side_effects=True, vmem_limit_bytes=53 << 20
        ),
        name="project_and_share",
    )(snapshots, pod_basis, penalty)
    normal, rhs, state, rates = pl.pallas_call(
        normal_equations,
        out_shape=[
            jax.ShapeDtypeStruct((OWN, F), jnp.float32),
            jax.ShapeDtypeStruct((R, OWN), jnp.float32),
            jax.ShapeDtypeStruct((1, 2, R), jnp.float32),
            jax.ShapeDtypeStruct((1, 2, R), jnp.float32),
        ],
        in_specs=[vmem] * 4,
        out_specs=[hbm] * 4,
        scratch_shapes=[
            pltpu.VMEM((2, 128, 128), jnp.float32),
            pltpu.VMEM((OWN, F), jnp.float32),
            pltpu.VMEM((R, OWN), jnp.float32),
            pltpu.VMEM((2, 1, 2, R), jnp.float32),
            pltpu.SemaphoreType.DMA((len(tiles()) + 3,)),
        ],
        compiler_params=pltpu.CompilerParams(vmem_limit_bytes=16 << 20),
        name="normal_equations",
    )(*shared)
    return normal, rhs.T, state, rates


def solution(mesh):
    return jax.shard_map(
        shards,
        mesh=mesh,
        in_specs=(P("tm", "space"), P(None, "space"), P()),
        out_specs=(P("tm", None), P("tm", None), P("tm", "space", None), P("tm", "space", None)),
        check_vma=False,
    )
```
